256 devices in a mesh: row: 16 (over y, z_lo), col: 16 (over x, z_hi, core).
Axes of the slice: x: 4, y: 4, z: 8 (z_hi: 2, z_lo: 4; z = z_hi * 4 + z_lo), core: 2. Of those that a mesh axis runs over, the one named last changes fastest.
Arguments:
- node_features: bfloat16 [16, 2048, 512], P('col', 'row'), may hold values from -6 to 6
- tile_coords: int32 [16, 16, 2, 128], P('row', 'col'), may hold values from 0 to 15, as said below
- tile_count: int32 [16, 16], P('row', 'col'), may hold values from 32 to 128, as said below
- tile_values: bfloat16 [16, 16, 128, 128, 128], P('row', 'col'), may hold values from -0.25 to 0.25
- weight: bfloat16 [512, 512], replicated, may hold values from -0.25 to 0.25
- cotangent: bfloat16 [16, 2048, 512], P('row', 'col'), may hold values from -6 to 6
Outputs:
- hidden: bfloat16 [16, 2048, 512], P('row', 'col')
- weight_grad: float32 [512, 512], replicated
- feature_grad: bfloat16 [16, 2048, 512], P('col', 'row')
The draws below stay inside these ranges and needn't reach their ends.
Inputs may be any that keep to these rules, and one draw needn't show every extreme that they name: In each block (i, j), slot k names tile row tile_coords[i, j, 0, k] below 16 and tile column tile_coords[i, j, 1, k] below 16; the 128 pairs of a block are distinct. `tile_count`: the number of used slots of each block; some block uses all 128.
All inputs are finite; a program needn't handle non-finite values.
Results may differ from the reference program's by a relative error of at most 0.028.
Values may be sent and summed in bfloat16 or wider, within the bound.
No kernel may reach another device: no remote copies, remote signals or barrier semaphores. Data moves between devices by JAX's collectives and lax.ppermute only.
A program may use at most 128 MiB of HBM per device.

```python
import math
import jax
import jax.numpy as jnp
from jax import lax

F = 512
TILE = 128
NODES = 32768
RB = 2048
CB = 2048
TR = 16
TC = 16
KMAX = 128
N_ROW = 16
N_COL = 16


def draw_tile_coords(key, part):
    key = jax.random.fold_in(key, 11)
    subkeys = jax.random.split(key, N_ROW * N_COL)

    def choose_tiles(subkey):
        shuffled = jax.random.permutation(subkey, TR * TC)[:KMAX]
        return jnp.stack([shuffled // TC, shuffled % TC])
    coords = jax.vmap(choose_tiles)(subkeys)
    return coords.reshape(N_ROW, N_COL, 2, KMAX).astype(jnp.int32)


def draw_tile_count(key, part):
    key = jax.random.fold_in(key, 23)
    draw_key, place_key = jax.random.split(key)
    counts = jax.random.randint(draw_key, (N_ROW * N_COL,), KMAX // 4, KMAX + 1)
    fullest = jax.random.randint(place_key, (), 0, N_ROW * N_COL)
    counts = jnp.where(jnp.arange(N_ROW * N_COL) == fullest, KMAX, counts)
    return counts.reshape(N_ROW, N_COL).astype(jnp.int32)


def steps_of(stream_key, dims, shards, low, largest):
    loudness, own = 1.0, jax.random.fold_in(stream_key, 6)
    for position, shards_of in shards:
        steps = jnp.exp(jax.random.uniform(jax.random.fold_in(own, position), (shards_of,), jnp.float32, low / len(shards), largest / len(shards)))
        loudness = loudness * jnp.repeat(steps, dims[position] // shards_of).reshape([-1 if axis == position else 1 for axis in range(len(dims))])
    return loudness


def scatter_about(key, dims, deviation, reach, cuts=(), kind=jnp.bfloat16):
    array = jax.random.normal(key, dims, jnp.float32) * deviation
    if len(cuts) > 0:
        array = steps_of(key, dims, cuts, -0.22, 0.18) * array
    return jnp.clip(array, min=-reach, max=reach).astype(kind)


def setup_inputs(seed: int = 0) -> dict:
    seeds = jax.random.split(jax.random.key(seed), 7)
    node_features = scatter_about(seeds[0], (N_COL, CB, F), 1.0, 6.0, ((0, 16), (1, 16)))
    tile_coords = draw_tile_coords(jax.random.fold_in(seeds[6], 71), 0)
    tile_count = draw_tile_count(jax.random.fold_in(seeds[6], 71), 0)
    tile_values = scatter_about(seeds[3], (N_ROW, N_COL, KMAX, TILE, TILE), (TILE * KMAX // (2 * TR)) ** -0.5, 0.25, ((0, 16), (1, 16)))
    weight = scatter_about(seeds[4], (F, F), F ** -0.5, 0.25)
    cotangent = scatter_about(seeds[5], (N_ROW, RB, F), 1.0, 6.0, ((0, 16), (1, 16)))
    return {"node_features": node_features, "tile_coords": tile_coords, "tile_count": tile_count, "tile_values": tile_values, "weight": weight, "cotangent": cotangent}


def silu_slope(pre):
    sigma = jax.nn.sigmoid(pre)
    return sigma * (1.0 + pre * (1.0 - sigma))

def forward_tiles(values, coords, count, source):
    usable = (jnp.arange(values.shape[0]) < count).astype(jnp.float32)
    pieces = source.reshape(TC, TILE, F)[coords[1]].astype(jnp.float32)
    product = jnp.einsum('kab,kbf->kaf', values.astype(jnp.float32), pieces) * usable[:, None, None]
    total = jnp.zeros((TR, TILE, F), jnp.float32).at[coords[0]].add(product)
    return total.reshape(RB, F)

def backward_tiles(values, coords, count, source):
    usable = (jnp.arange(values.shape[0]) < count).astype(jnp.float32)
    pieces = source.reshape(TR, TILE, F)[coords[0]].astype(jnp.float32)
    product = jnp.einsum('kab,kaf->kbf', values.astype(jnp.float32), pieces) * usable[:, None, None]
    total = jnp.zeros((TC, TILE, F), jnp.float32).at[coords[1]].add(product)
    return total.reshape(CB, F)

def reference(node_features, tile_coords, tile_count, tile_values, weight, cotangent):

    def row_total(index):

        def advance(total, column):
            part = forward_tiles(tile_values[index, column], tile_coords[index, column], tile_count[index, column], node_features[column])
            rounded = lax.optimization_barrier(part.astype(jnp.bfloat16))
            return (total + rounded.astype(jnp.float32), None)
        total, _ = lax.scan(advance, jnp.zeros((RB, F), jnp.float32), jnp.arange(N_COL))
        return total.astype(jnp.bfloat16)
    summed = lax.map(row_total, jnp.arange(N_ROW)).reshape(NODES, F)
    pre = jnp.dot(summed, weight, preferred_element_type=jnp.float32)
    hidden = jax.nn.silu(pre).astype(jnp.bfloat16)
    grad_pre = (cotangent.reshape(NODES, F).astype(jnp.float32) * silu_slope(pre)).astype(jnp.bfloat16)
    grad_summed = jnp.dot(grad_pre, weight.T, preferred_element_type=jnp.float32).astype(jnp.bfloat16)
    weight_grad = jnp.dot(summed.T, grad_pre, preferred_element_type=jnp.float32) / math.sqrt(NODES)
    grad_blocks = grad_summed.reshape(N_ROW, RB, F)

    def column_total(column):

        def advance(total, index):
            part = backward_tiles(tile_values[index, column], tile_coords[index, column], tile_count[index, column], grad_blocks[index])
            rounded = lax.optimization_barrier(part.astype(jnp.bfloat16))
            return (total + rounded.astype(jnp.float32), None)
        total, _ = lax.scan(advance, jnp.zeros((CB, F), jnp.float32), jnp.arange(N_ROW))
        return total.astype(jnp.bfloat16)
    feature_grad = lax.map(column_total, jnp.arange(N_COL))
    return (hidden.reshape(N_ROW, RB, F), weight_grad, feature_grad)
```

```python
import math

import jax
import jax.numpy as jnp
from jax import lax
from jax.experimental import pallas as pl
from jax.experimental.pallas import tpu as pltpu
from jax.sharding import PartitionSpec as P

Y = 4
Z = 4
X = 4
H = 2
C = 2
TILE = 128


def row_shift(data, axis, step):
    pairs = []
    for r in range(Y * Z):
        y, z = divmod(r, Z)
        if axis == "y":
            source = (y + step) % Y * Z + z
        else:
            source = y * Z + (z + step) % Z
        pairs.append((source, r))
    return lax.ppermute(data, "row", pairs)


def col_shift(data, axis, step):
    pairs = []
    for c in range(X * H * C):
        x, h, k = c // (H * C), c // C % H, c % C
        if axis == "x":
            x = (x + step) % X
        elif axis == "h":
            h = (h + step) % H
        else:
            k = (k + step) % C
        pairs.append(((x * H + h) * C + k, c))
    return lax.ppermute(data, "col", pairs)


def densify_kernel(place_ref, count_ref, values_ref, forward_ref, backward_ref):
    size = forward_ref.shape[0]
    zeros = jnp.zeros((TILE, size), forward_ref.dtype)

    def clear(i, _):
        rows = pl.ds(pl.multiple_of(i * TILE, TILE), TILE)
        forward_ref[rows, :] = zeros
        backward_ref[rows, :] = zeros
        return 0

    lax.fori_loop(0, size // TILE, clear, 0)

    def put(k, _):
        r = pl.ds(pl.multiple_of(place_ref[0, k] * TILE, TILE), TILE)
        c = pl.ds(pl.multiple_of(place_ref[1, k] * TILE, TILE), TILE)
        tile = values_ref[k]
        forward_ref[r, c] = tile
        backward_ref[c, r] = tile.T
        return 0

    lax.fori_loop(0, count_ref[0], put, 0)


def densify(values, place, count):
    size = 16 * TILE
    dense = jax.ShapeDtypeStruct((size, size), values.dtype)
    return pl.pallas_call(
        densify_kernel,
        out_shape=(dense, dense),
        in_specs=[
            pl.BlockSpec(memory_space=pltpu.SMEM),
            pl.BlockSpec(memory_space=pltpu.SMEM),
            pl.BlockSpec(memory_space=pltpu.VMEM),
        ],
        out_specs=(
            pl.BlockSpec(memory_space=pltpu.VMEM),
            pl.BlockSpec(memory_space=pltpu.VMEM),
        ),
        compiler_params=pltpu.CompilerParams(vmem_limit_bytes=40 * 1024 * 1024),
        cost_estimate=pl.CostEstimate(
            flops=0, bytes_accessed=20 * 1024 * 1024, transcendentals=0
        ),
    )(place, count, values)


def f32(value):
    return value.astype(jnp.float32)


def bf16(value):
    return value.astype(jnp.bfloat16)


def matmul(a, b):
    return jnp.dot(a, b, preferred_element_type=jnp.float32)


def body(node_features, tile_coords, tile_count, tile_values, weight, cotangent):
    features = node_features[0]
    me_row = lax.axis_index("row")
    me_col = lax.axis_index("col")
    my, mz = me_row // Z, me_row % Z
    mx, mh, mk = me_col // (H * C), me_col // C % H, me_col % C
    nodes_all = TILE * Y * Z * X * H * C

    tr, tc = tile_coords[0, 0, 0], tile_coords[0, 0, 1]
    place_r = ((tr + mk) % C) * (X * H) + ((tr // (H * C) - mx) % X) * H + (tr // C + mh) % H
    place_c = ((tc // Z - my) % Y) * Z + (tc - mz) % Z
    forward, backward = densify(
        tile_values[0, 0], jnp.stack([place_r, place_c]), tile_count[0]
    )

    run = jnp.concatenate([features] + [row_shift(features, "z", s) for s in (1, 2, 3)])
    source = jnp.concatenate([run] + [row_shift(run, "y", s) for s in (1, 2, 3)])

    half = 8 * TILE
    away = bf16(matmul(forward[half:], source))
    home = matmul(forward[:half], source)
    home = bf16(home + f32(col_shift(away, "k", 1)))
    quarter = 2 * TILE
    total = f32(home[:quarter])
    for s in (1, 2, 3):
        total += f32(col_shift(home[s * quarter : (s + 1) * quarter], "x", X - s))
    summed = bf16(total[:TILE] + f32(col_shift(bf16(total[TILE:]), "h", 1)))

    pre = matmul(summed, weight)
    sigma = jax.nn.sigmoid(pre)
    hidden = bf16(pre * sigma)
    grad_pre = bf16(f32(cotangent[0]) * (sigma * (1.0 + pre * (1.0 - sigma))))
    grad_summed = bf16(
        lax.dot_general(
            grad_pre, weight, (((1,), (1,)), ((), ())), preferred_element_type=jnp.float32
        )
    )
    term = lax.dot_general(
        summed, grad_pre, (((0,), (0,)), ((), ())), preferred_element_type=jnp.float32
    )

    pair = jnp.concatenate([grad_summed, col_shift(grad_summed, "h", 1)])
    eight = jnp.concatenate([pair] + [col_shift(pair, "x", s) for s in (1, 2, 3)])
    grads = jnp.concatenate([eight, col_shift(eight, "k", 1)])

    def cut(value, index, size):
        return lax.dynamic_slice_in_dim(value, index * size, size, 0)

    part = cut(term, mk, 256) + f32(col_shift(bf16(cut(term, 1 - mk, 256)), "k", 1))
    piece = cut(part, mx, 64)
    for s in (1, 2, 3):
        piece += f32(col_shift(bf16(cut(part, (mx + s) % X, 64)), "x", X - s))
    piece = cut(piece, mh, 32) + f32(col_shift(bf16(cut(piece, 1 - mh, 32)), "h", 1))
    for axis, me in (("y", my), ("z", mz)):
        sent = bf16(piece)
        parts = [sent] + [row_shift(sent, axis, s) for s in (1, 2, 3)]
        ordered = lax.dynamic_slice_in_dim(jnp.stack(parts + parts[:3]), (4 - me) % 4, 4, 0)
        piece = f32(ordered[0]) + f32(ordered[1]) + f32(ordered[2]) + f32(ordered[3])
    sent = bf16(piece / math.sqrt(nodes_all))
    other = col_shift(sent, "h", 1)
    sent = jnp.where(mh == 0, jnp.concatenate([sent, other]), jnp.concatenate([other, sent]))
    parts = [sent] + [col_shift(sent, "x", s) for s in (1, 2, 3)]
    sent = lax.dynamic_slice_in_dim(
        jnp.concatenate(parts + parts[:3]), ((X - mx) % X) * 64, 256, 0
    )
    other = col_shift(sent, "k", 1)
    weight_grad = f32(
        jnp.where(mk == 0, jnp.concatenate([sent, other]), jnp.concatenate([other, sent]))
    )

    block = Z * TILE
    got = []
    for s in (2, 1, 3):
        back = bf16(matmul(backward[s * block : (s + 1) * block], grads))
        got.append(row_shift(back, "y", Y - s))
    total = matmul(backward[:block], grads)
    for arrived in got:
        total += f32(arrived)
    result = total[:TILE]
    for s in (1, 2, 3):
        result += f32(row_shift(bf16(total[s * TILE : (s + 1) * TILE]), "z", Z - s))
    return (hidden[None], weight_grad, bf16(result)[None])


def solution(mesh):
    in_specs = (
        P("col", "row", None),
        P("row", "col", None, None),
        P("row", "col"),
        P("row", "col", None, None, None),
        P(),
        P("row", "col", None),
    )
    out_specs = (P("row", "col", None), P(), P("col", "row", None))
    return jax.shard_map(body, mesh=mesh, in_specs=in_specs, out_specs=out_specs, check_vma=False)
```

```python
import functools
import math

import jax
import jax.numpy as jnp
from jax import lax
from jax.experimental import pallas as pl
from jax.experimental.pallas import tpu as pltpu
from jax.sharding import PartitionSpec as P

Y = 4
Z = 4
X = 4
H = 2
C = 2
TILE = 128
VMEM_LIMIT = 4 * 1024 * 1024
BF16 = jnp.bfloat16
F32 = jnp.float32


def row_shift(data, axis, step):
    pairs = []
    for r in range(Y * Z):
        y, z = divmod(r, Z)
        if axis == "y":
            source = (y + step) % Y * Z + z
        else:
            source = y * Z + (z + step) % Z
        pairs.append((source, r))
    return lax.ppermute(data, "row", pairs)


def col_shift(data, axis, step):
    pairs = []
    for c in range(X * H * C):
        x, h, k = c // (H * C), c // C % H, c % C
        if axis == "x":
            x = (x + step) % X
        elif axis == "h":
            h = (h + step) % H
        else:
            k = (k + step) % C
        pairs.append(((x * H + h) * C + k, c))
    return lax.ppermute(data, "col", pairs)


def densify_kernel(transpose, firsts, place_ref, count_ref, values_ref, *dense_refs):
    size = dense_refs[0].shape[0]

    def clear(i, _):
        rows = pl.ds(pl.multiple_of(i * TILE, TILE), TILE)
        for ref in dense_refs:
            ref[rows, :] = jnp.zeros((TILE, ref.shape[1]), ref.dtype)
        return 0

    lax.fori_loop(0, size // TILE, clear, 0)

    def put(k, _):
        r, c = place_ref[0, k], place_ref[1, k]
        if transpose:
            r, c = c, r
        for first, ref in zip(firsts, dense_refs):

            @pl.when((c >= first) & (c < first + ref.shape[1] // TILE))
            def _():
                rows = pl.ds(pl.multiple_of(r * TILE, TILE), TILE)
                columns = pl.ds(pl.multiple_of((c - first) * TILE, TILE), TILE)
                tile = values_ref[k]
                ref[rows, columns] = tile.T if transpose else tile

        return 0

    lax.fori_loop(0, count_ref[0], put, 0)


def densify(values, place, count, transpose, *parts):
    size = 16 * TILE
    vmem = pl.BlockSpec(memory_space=pltpu.VMEM)
    return pl.pallas_call(
        functools.partial(densify_kernel, transpose, [first for first, _ in parts]),
        out_shape=[
            jax.ShapeDtypeStruct((size, (last - first) * TILE), values.dtype)
            for first, last in parts
        ],
        in_specs=[
            pl.BlockSpec(memory_space=pltpu.SMEM),
            pl.BlockSpec(memory_space=pltpu.SMEM),
            vmem,
        ],
        out_specs=[vmem] * len(parts),
        compiler_params=pltpu.CompilerParams(vmem_limit_bytes=VMEM_LIMIT),
        cost_estimate=pl.CostEstimate(
            flops=0, bytes_accessed=12 * 1024 * 1024, transcendentals=0
        ),
    )(place, count, values)


def products_kernel(pieces, has_added, dense_ref, source_ref, *refs):
    outs = refs[1:] if has_added else refs
    for (first, last, _), out_ref in zip(pieces, outs):
        start = first * TILE
        while start < last * TILE:
            stop = min(start + 4 * TILE, last * TILE)
            total = jnp.dot(
                dense_ref[start:stop, :], source_ref[...], preferred_element_type=jnp.float32
            )
            if has_added:
                total += refs[0][start:stop, :]
            out_ref[start - first * TILE : stop - first * TILE, :] = total.astype(out_ref.dtype)
            start = stop


def products(dense, source, added, pieces):
    width = source.shape[1]
    operands = [dense, source] + ([] if added is None else [added])
    vmem = pl.BlockSpec(memory_space=pltpu.VMEM)
    tiles = sum(last - first for first, last, _ in pieces)
    return pl.pallas_call(
        functools.partial(products_kernel, pieces, added is not None),
        out_shape=[
            jax.ShapeDtypeStruct(((last - first) * TILE, width), dtype)
            for first, last, dtype in pieces
        ],
        in_specs=[vmem] * len(operands),
        out_specs=[vmem] * len(pieces),
        compiler_params=pltpu.CompilerParams(vmem_limit_bytes=VMEM_LIMIT),
        cost_estimate=pl.CostEstimate(
            flops=2 * tiles * TILE * width * dense.shape[1],
            bytes_accessed=tiles * TILE * (dense.shape[1] + width) * 4,
            transcendentals=0,
        ),
    )(*operands)


def f32(value):
    return value.astype(jnp.float32)


def bf16(value):
    return value.astype(jnp.bfloat16)


def matmul(a, b):
    return jnp.dot(a, b, preferred_element_type=jnp.float32)


def join(*values):
    return lax.optimization_barrier(values)


def from_z(data):
    return [row_shift(data, "z", s) for s in (1, 2, 3)]


def from_y(data):
    return [row_shift(data, "y", s) for s in (1, 2, 3)]


def from_x(data):
    return [col_shift(data, "x", s) for s in (1, 2, 3)]


def rows_of(data, first, last):
    return data[first * TILE : last * TILE]


def total_of(own, parts):
    total = f32(own)
    for part in parts:
        total += f32(part)
    return total


def cut(value, index, size):
    return lax.dynamic_slice_in_dim(value, index * size, size, 0)


def sum_of_four(parts):
    return (f32(parts[0]) + f32(parts[2])) + (f32(parts[1]) + f32(parts[3]))


def assemble_kernel(scale, me_ref, own_ref, other_ref, out_ref):
    rows = own_ref.shape[0] // X
    for s in range(X):
        first = (me_ref[0] + s & 3) * C * rows
        for ref, core in ((own_ref, me_ref[1]), (other_ref, 1 - me_ref[1])):
            place = pl.ds(pl.multiple_of(first + core * rows, rows), rows)
            out_ref[place, :] = ref[s * rows : (s + 1) * rows, :].astype(F32) * scale


def assemble(me, own, other, scale):
    vmem = pl.BlockSpec(memory_space=pltpu.VMEM)
    return pl.pallas_call(
        functools.partial(assemble_kernel, scale),
        out_shape=jax.ShapeDtypeStruct((2 * own.shape[0], own.shape[1]), F32),
        in_specs=[pl.BlockSpec(memory_space=pltpu.SMEM), vmem, vmem],
        out_specs=vmem,
        compiler_params=pltpu.CompilerParams(vmem_limit_bytes=VMEM_LIMIT),
    )(me, own, other)


def body(node_features, tile_coords, tile_count, tile_values, weight, cotangent):
    features = node_features[0]
    me_row = lax.axis_index("row")
    me_col = lax.axis_index("col")
    my, mz = me_row >> 2, me_row & 3
    mx, mh, mk = me_col >> 2, me_col >> 1 & 1, me_col & 1
    nodes_all = TILE * Y * Z * X * H * C
    full = features.shape[1]

    tr, tc = tile_coords[0, 0, 0], tile_coords[0, 0, 1]
    place_r = ((tr >> 1) + mh & 1) * 8 + (tr + mk & 1) * 4 + ((tr >> 2) - mx & 3)
    far_y, far_z = (tc >> 2) - my & 3, tc - mz & 3
    place_c = jnp.where(
        far_y == 0, far_z, jnp.where(far_z == 0, 3 + far_y, 3 + far_y * 3 + far_z)
    )
    place = jnp.stack([place_r, place_c])
    values, count = tile_values[0, 0], tile_count[0]

    along_y = from_y(features)
    along_z, forward, place = join(
        from_z(features),
        densify(values, place, count, False, (0, 7), (7, 16)),
        place,
    )
    rest = jnp.concatenate(along_z)
    near = jnp.concatenate([features, rest] + along_y)
    along_y, near, backward1, place = join(
        from_y(rest),
        products(forward[0], near, None, [(0, 16, F32)])[0],
        densify(values, place, count, True, (0, 8))[0],
        place,
    )
    far = jnp.concatenate(along_y)

    (away,) = products(forward[1], far, near, [(12, 16, BF16)])
    away, far = join(away, far)
    arrived = col_shift(away, "k", 1)
    home, away, own = products(
        forward[1], far, near, [(8, 12, F32), (4, 8, BF16), (0, 4, F32)]
    )
    home, arrived, away, own = join(home, arrived, away, own)
    lead = [bf16(rows_of(home, s, s + 1) + f32(rows_of(arrived, s, s + 1))) for s in range(X)]
    lead_parts = [col_shift(lead[s], "x", X - s) for s in (1, 2, 3)]
    lead, lead_parts, arrived, place = join(
        lead[0], lead_parts, col_shift(away, "k", 1), place
    )
    lead = bf16(total_of(lead, lead_parts))
    own = [rows_of(own, s, s + 1) + f32(rows_of(arrived, s, s + 1)) for s in range(X)]
    lead = col_shift(lead, "h", 1)
    own_parts = [col_shift(bf16(own[s]), "x", X - s) for s in (1, 2, 3)]
    own_parts, own, backward2 = join(
        own_parts, own[0], densify(values, place, count, True, (8, 16))[0]
    )
    summed = bf16(total_of(own, [lead] + own_parts))

    pre = matmul(summed, weight)
    sigma = jax.nn.sigmoid(pre)
    hidden = bf16(pre * sigma)
    grad_pre = bf16(f32(cotangent[0]) * (sigma * (1.0 + pre * (1.0 - sigma))))
    grad_summed = bf16(
        lax.dot_general(
            grad_pre, weight, (((1,), (1,)), ((), ())), preferred_element_type=jnp.float32
        )
    )
    term = lax.dot_general(
        summed, grad_pre, (((0,), (0,)), ((), ())), preferred_element_type=jnp.float32
    )

    other = col_shift(grad_summed, "h", 1)
    own_parts = from_x(grad_summed)
    own_parts, term = join(own_parts, term)
    w_parts = [col_shift(bf16(cut(term, mx + X - s & 3, 128)), "x", s) for s in (1, 2, 3)]
    own = jnp.concatenate([grad_summed] + own_parts)
    own_core = col_shift(own, "k", 1)
    other_parts = from_x(other)
    w = total_of(cut(term, mx, 128), w_parts)
    w = cut(w, mk, 64) + f32(col_shift(bf16(cut(w, 1 - mk, 64)), "k", 1))
    near = products(backward1, jnp.concatenate([own, own_core]), None, [(0, 16, F32)])[0]
    (w,) = join(bf16(w))
    other_parts, near, w_parts = join(other_parts, near, from_y(w))
    other = jnp.concatenate([other] + other_parts)
    other_core = col_shift(other, "k", 1)
    other_core, w = join(other_core, bf16(sum_of_four([w] + w_parts)))

    *lead, near1, near2, near3, run, own = products(
        backward2,
        jnp.concatenate([other, other_core]),
        near,
        [(7, 10, BF16), (10, 13, BF16), (13, 16, BF16)]
        + [(4, 5, BF16), (5, 6, BF16), (6, 7, BF16), (1, 4, F32), (0, 1, F32)],
    )
    lead, near, run, own, w = join(lead, [near1, near2, near3], run, own, w)
    w_parts = from_z(w)
    (w,) = join(bf16(sum_of_four([w] + w_parts)))
    lead_parts = [row_shift(lead[s - 1], "y", Y - s) for s in (1, 2, 3)]
    lead_parts, w_part = join(lead_parts, col_shift(w, "h", 1))
    run = [rows_of(run, s, s + 1) for s in range(3)]
    for s in range(3):
        run[s] = bf16(total_of(run[s], [rows_of(part, s, s + 1) for part in lead_parts]))
    z_parts = [row_shift(run[s - 1], "z", Z - s) for s in (1, 2, 3)]
    near_parts = [row_shift(near[s - 1], "y", Y - s) for s in (1, 2, 3)]
    (w,) = join(bf16(f32(w) + f32(w_part)))
    z_parts, near_parts, w_parts = join(z_parts, near_parts, from_x(w))
    feature_grad = bf16(total_of(own, near_parts + z_parts))

    parts = jnp.concatenate([w] + w_parts)
    weight_grad = assemble(
        jnp.stack([mx, mk]), parts, col_shift(parts, "k", 1), 1.0 / math.sqrt(nodes_all)
    )
    return (hidden[None], weight_grad, feature_grad[None])


def solution(mesh):
    in_specs = (
        P("col", "row", None),
        P("row", "col", None, None),
        P("row", "col"),
        P("row", "col", None, None, None),
        P(),
        P("row", "col", None),
    )
    out_specs = (P("row", "col", None), P(), P("col", "row", None))
    return jax.shard_map(body, mesh=mesh, in_specs=in_specs, out_specs=out_specs, check_vma=False)
```

```python
import functools
import math

import jax
import jax.numpy as jnp
from jax import lax
from jax.experimental import pallas as pl
from jax.experimental.pallas import tpu as pltpu
from jax.sharding import PartitionSpec as P

Y = 4
Z = 4
X = 4
H = 2
C = 2
TILE = 128
VMEM_LIMIT = 4 * 1024 * 1024
BF16 = jnp.bfloat16
F32 = jnp.float32


def row_shift(data, axis, step):
    pairs = []
    for r in range(Y * Z):
        y, z = divmod(r, Z)
        if axis == "y":
            source = (y + step) % Y * Z + z
        else:
            source = y * Z + (z + step) % Z
        pairs.append((source, r))
    return lax.ppermute(data, "row", pairs)


def col_shift(data, axis, step):
    pairs = []
    for c in range(X * H * C):
        x, h, k = c // (H * C), c // C % H, c % C
        if axis == "x":
            x = (x + step) % X
        elif axis == "h":
            h = (h + step) % H
        else:
            k = (k + step) % C
        pairs.append(((x * H + h) * C + k, c))
    return lax.ppermute(data, "col", pairs)


def densify_kernel(
    firsts, place_ref, count_ref, values_ref, *refs
):
    *dense_refs, held_ref, sems = refs
    size = dense_refs[0].shape[0]
    part = held_ref.shape[1]
    parts = values_ref.shape[0] // part

    def copy(i):
        return pltpu.make_async_copy(
            values_ref.at[pl.ds(i * part, part)], held_ref.at[i % 2], sems.at[i % 2]
        )

    copy(0).start()

    def clear(i, _):
        rows = pl.ds(pl.multiple_of(i * TILE, TILE), TILE)
        for ref in dense_refs:
            ref[rows, :] = jnp.zeros((TILE, ref.shape[1]), ref.dtype)
        return 0

    lax.fori_loop(0, size // TILE, clear, 0)

    for i in range(parts):
        if i + 1 < parts:
            copy(i + 1).start()
        copy(i).wait()

        def put(k, _):
            r, c = place_ref[0, i * part + k], place_ref[1, i * part + k]
            for first, ref in zip(firsts, dense_refs):

                @pl.when((c >= first) & (c < first + ref.shape[1] // TILE))
                def _():
                    rows = pl.ds(pl.multiple_of(r * TILE, TILE), TILE)
                    columns = pl.ds(pl.multiple_of((c - first) * TILE, TILE), TILE)
                    ref[rows, columns] = held_ref[i % 2, k]

            return 0

        lax.fori_loop(0, jnp.clip(count_ref[0] - i * part, 0, part), put, 0)


def densify(values, place, count, *parts):
    size = 16 * TILE
    vmem = pl.BlockSpec(memory_space=pltpu.VMEM)
    return pl.pallas_call(
        functools.partial(densify_kernel, [first for first, _ in parts]),
        out_shape=[
            jax.ShapeDtypeStruct((size, (last - first) * TILE), values.dtype)
            for first, last in parts
        ],
        in_specs=[
            pl.BlockSpec(memory_space=pltpu.SMEM),
            pl.BlockSpec(memory_space=pltpu.SMEM),
            pl.BlockSpec(memory_space=pltpu.HBM),
        ],
        out_specs=[vmem] * len(parts),
        scratch_shapes=[
            pltpu.VMEM((2, 16, TILE, TILE), values.dtype),
            pltpu.SemaphoreType.DMA((2,)),
        ],
        compiler_params=pltpu.CompilerParams(vmem_limit_bytes=VMEM_LIMIT),
        cost_estimate=pl.CostEstimate(
            flops=0, bytes_accessed=12 * 1024 * 1024, transcendentals=0
        ),
    )(place, count, values)


def products_kernel(pieces, has_added, dense_ref, source_ref, *refs):
    outs = refs[1:] if has_added else refs
    for (first, last, _), out_ref in zip(pieces, outs):
        start = first * TILE
        while start < last * TILE:
            stop = min(start + 4 * TILE, last * TILE)
            total = jnp.dot(
                dense_ref[start:stop, :],
                source_ref[...],
                preferred_element_type=jnp.float32,
            )
            if has_added:
                total += refs[0][start:stop, :]
            out_ref[start - first * TILE : stop - first * TILE, :] = total.astype(out_ref.dtype)
            start = stop


def products(dense, source, added, pieces):
    width = source.shape[1]
    operands = [dense, source] + ([] if added is None else [added])
    vmem = pl.BlockSpec(memory_space=pltpu.VMEM)
    tiles = sum(last - first for first, last, _ in pieces)
    return pl.pallas_call(
        functools.partial(products_kernel, pieces, added is not None),
        out_shape=[
            jax.ShapeDtypeStruct(((last - first) * TILE, width), dtype)
            for first, last, dtype in pieces
        ],
        in_specs=[vmem] * len(operands),
        out_specs=[vmem] * len(pieces),
        compiler_params=pltpu.CompilerParams(vmem_limit_bytes=VMEM_LIMIT),
        cost_estimate=pl.CostEstimate(
            flops=2 * tiles * TILE * width * dense.shape[1],
            bytes_accessed=tiles * TILE * (dense.shape[1] + width) * 4,
            transcendentals=0,
        ),
    )(*operands)


def f32(value):
    return value.astype(jnp.float32)


def bf16(value):
    return value.astype(jnp.bfloat16)


def matmul(a, b):
    return jnp.dot(a, b, preferred_element_type=jnp.float32)


def join(*values):
    return lax.optimization_barrier(values)


def from_z(data):
    return [row_shift(data, "z", s) for s in (1, 2, 3)]


def from_y(data):
    return [row_shift(data, "y", s) for s in (1, 2, 3)]


def from_x(data):
    return [col_shift(data, "x", s) for s in (1, 2, 3)]


def rows_of(data, first, last):
    return data[first * TILE : last * TILE]


def total_of(own, parts):
    total = f32(own)
    for part in parts:
        total += f32(part)
    return total


def cut(value, index, size):
    return lax.dynamic_slice_in_dim(value, index * size, size, 0)


def call(kernel, outs, *operands, scratch=(), scalars=0, flops=0):
    vmem = pl.BlockSpec(memory_space=pltpu.VMEM)
    shapes = [jax.ShapeDtypeStruct(shape, dtype) for shape, dtype in outs]
    return pl.pallas_call(
        kernel,
        out_shape=shapes,
        in_specs=[pl.BlockSpec(memory_space=pltpu.SMEM)] * scalars
        + [vmem] * (len(operands) - scalars),
        out_specs=[vmem] * len(outs),
        scratch_shapes=list(scratch),
        compiler_params=pltpu.CompilerParams(vmem_limit_bytes=VMEM_LIMIT),
        cost_estimate=pl.CostEstimate(
            flops=flops, bytes_accessed=4 * 1024 * 1024, transcendentals=0
        ),
    )(*operands)


def split_for_x(me_x, both_ref, outs):
    full = both_ref.shape[0] // 2
    for s, ref in enumerate(outs):
        first = pl.multiple_of(full + ((me_x - s) & 3) * TILE, TILE)
        ref[:full, :] = both_ref[:full, :]
        ref[full:, :] = both_ref[pl.ds(first, TILE), :]


def middle_kernel(
    me_ref, own_ref, p0, p1, p2, p3, weight_ref, cotangent_ref, hidden_ref, both_ref, *outs
):
    full = weight_ref.shape[0]
    total = own_ref[...] + f32(p0[...]) + f32(p1[...]) + f32(p2[...]) + f32(p3[...])
    summed = bf16(total)
    both_ref[full:, :] = summed.T
    pre = matmul(summed, weight_ref[...])
    sigma = 1.0 / (1.0 + jnp.exp(-pre))
    hidden_ref[...] = bf16(pre * sigma)
    slope = sigma * (1.0 + pre * (1.0 - sigma))
    both_ref[:full, :] = bf16(f32(cotangent_ref[...]) * slope).T
    split_for_x(me_ref[0], both_ref, outs)


def split_kernel(me_ref, both_ref, *outs):
    split_for_x(me_ref[0], both_ref, outs)


def first_kernel(dense1_ref, dense2_ref, source_ref, near_ref, far_ref):
    rows, nodes = near_ref.shape[0], source_ref.shape[1]
    for dense_ref, ref in ((dense1_ref, near_ref), (dense2_ref, far_ref)):
        for first in range(0, ref.shape[1], 3 * TILE):
            span = slice(first, min(first + 3 * TILE, ref.shape[1]))
            ref[:, span] = matmul(source_ref[:rows, :], dense_ref[:nodes, span])


def lead_kernel(me_ref, dense_ref, source_ref, first_ref, added_ref, *refs):
    lead1, over1, lead2, over3, lead3, w_ref, *totals = refs
    full, nodes = lead1.shape[0], source_ref.shape[1]
    for ref, total_ref in zip((first_ref, source_ref), totals):
        total_ref[...] = lax.dot_general(
            ref[full:, :],
            ref[:full, :],
            (((1,), (1,)), ((), ())),
            preferred_element_type=jnp.float32,
        )
    rows = w_ref.shape[0] * TILE // full
    span = pl.ds(pl.multiple_of(me_ref[1] * rows, rows), rows)
    w = bf16(totals[0][span, :] + totals[1][span, :])
    for i in range(full // TILE):
        w_ref[i * rows : (i + 1) * rows, :] = w[:, i * TILE : (i + 1) * TILE]
    middle = (over1, lead2, over3)
    for first, outs in ((0, (lead1,)), (6, (lead3,)), (3, middle)):
        span = slice(first * TILE, (first + 3) * TILE)
        total = bf16(matmul(source_ref[:full, :], dense_ref[nodes:, span]) + added_ref[:, span])
        width = 3 * TILE // len(outs)
        for i, ref in enumerate(outs):
            ref[:full, :] = total[:, i * width : (i + 1) * width]
    for ref in (over1, over3):
        ref[full:, :] = w_ref[...]


def rest_kernel(dense_ref, source_ref, added_ref, across_ref, w0_ref, w2_ref, *refs):
    near1, near2, near3, run, own, pair = refs
    full, nodes = own.shape[0], source_ref.shape[1]
    pair[...] = f32(w0_ref[...]) + f32(w2_ref[...])
    for first, last, outs in ((0, 4, (own, run)), (4, 7, (near1, near2, near3))):
        span = slice(first * TILE, last * TILE)
        total = matmul(source_ref[:full, :], dense_ref[nodes:, span]) + added_ref[:, span]
        start = 0
        for ref in outs:
            ref[...] = total[:, start : start + ref.shape[1]].astype(ref.dtype)
            start += ref.shape[1]
    run[:, TILE : 2 * TILE] += f32(across_ref[...])


def combine_kernel(
    run, near1, near2, near3, pair, down, up, over1, over3, z1, z2, z3, y1, y2, y3, w_out
):
    full = run.shape[0]
    for s, ref in enumerate((z1, z2, z3)):
        span = slice(s * TILE, (s + 1) * TILE)
        ref[...] = bf16(run[:, span] + f32(down[:, span]) + f32(up[:, span]))
    y1[:full, :] = near1[...]
    y2[:full, :] = bf16(near2[...] + f32(over1[:full, :]) + f32(over3[:full, :]))
    y3[:full, :] = near3[...]
    total = bf16(pair[...] + (f32(over1[full:, :]) + f32(over3[full:, :])))
    for ref in (y1, y2, y3):
        ref[full:, :] = total
    w_out[...] = total


def sum_of_four(parts):
    return (f32(parts[0]) + f32(parts[2])) + (f32(parts[1]) + f32(parts[3]))


def assemble_kernel(scale, me_ref, own_ref, other_ref, out_ref):
    parts = out_ref.shape[1] // TILE
    rows = own_ref.shape[0] // X // parts
    for s in range(X):
        first = (me_ref[0] + s & 3) * C * rows
        for ref, core in ((own_ref, me_ref[1]), (other_ref, 1 - me_ref[1])):
            place = pl.ds(pl.multiple_of(first + core * rows, rows), rows)
            for i in range(parts):
                start = (s * parts + i) * rows
                piece = ref[start : start + rows, :].astype(F32)
                out_ref[place, i * TILE : (i + 1) * TILE] = piece * scale


def assemble(me, own, other, scale, full):
    vmem = pl.BlockSpec(memory_space=pltpu.VMEM)
    return pl.pallas_call(
        functools.partial(assemble_kernel, scale),
        out_shape=jax.ShapeDtypeStruct((full, full), F32),
        in_specs=[pl.BlockSpec(memory_space=pltpu.SMEM), vmem, vmem],
        out_specs=vmem,
        compiler_params=pltpu.CompilerParams(vmem_limit_bytes=VMEM_LIMIT),
    )(me, own, other)


def body(node_features, tile_coords, tile_count, tile_values, weight, cotangent):
    features = node_features[0]
    me_row = lax.axis_index("row")
    me_col = lax.axis_index("col")
    my, mz = me_row >> 2, me_row & 3
    mx, mh, mk = me_col >> 2, me_col >> 1 & 1, me_col & 1
    nodes_all = TILE * Y * Z * X * H * C
    full = features.shape[1]

    tr, tc = tile_coords[0, 0, 0], tile_coords[0, 0, 1]
    place_r = ((tr >> 1) + mh & 1) * 8 + (tr + mk & 1) * 4 + ((tr >> 2) - mx & 3)
    far_y, far_z = (tc >> 2) - my & 3, tc - mz & 3
    place_c = jnp.where(
        far_y == 0, far_z, jnp.where(far_z == 0, 3 + far_y, 3 + far_y * 3 + far_z)
    )
    place = jnp.stack([place_r, place_c])
    values, count = tile_values[0, 0], tile_count[0]

    along_y = from_y(features)
    along_z, along_y[1], forward = join(
        from_z(features), along_y[1], densify(values, place, count, (0, 7), (7, 16))
    )
    rest = jnp.concatenate(along_z)
    near = jnp.concatenate([features, rest] + along_y)
    far = [row_shift(rest, "y", 1), row_shift(rest, "y", 3)]
    far += [row_shift(along_y[1], "z", 1), row_shift(along_y[1], "z", 3)]
    far += [row_shift(along_z[1], "y", 2)]
    far, near = join(far, products(forward[0], near, None, [(0, 16, F32)])[0])
    far = jnp.concatenate([far[0], far[2], far[4], far[3], far[1]])

    (away,) = products(forward[1], far, near, [(12, 16, BF16)])
    away, far = join(away, far)
    arrived = col_shift(away, "k", 1)
    home, away, own = products(
        forward[1], far, near, [(8, 12, F32), (4, 8, BF16), (0, 4, F32)]
    )
    home, arrived, away, own = join(home, arrived, away, own)
    lead = [bf16(rows_of(home, s, s + 1) + f32(rows_of(arrived, s, s + 1))) for s in range(X)]
    lead_parts = [col_shift(lead[s], "x", X - s) for s in (1, 2, 3)]
    lead, lead_parts, arrived = join(lead[0], lead_parts, col_shift(away, "k", 1))
    lead = bf16(total_of(lead, lead_parts))
    own = [rows_of(own, s, s + 1) + f32(rows_of(arrived, s, s + 1)) for s in range(X)]
    lead = col_shift(lead, "h", 1)
    own_parts = [col_shift(bf16(own[s]), "x", X - s) for s in (1, 2, 3)]
    me = jnp.stack([mx, mk])
    wider = full + TILE
    hidden, both, *own_sent = call(
        middle_kernel,
        [((TILE, full), BF16), ((2 * full, TILE), BF16)] + [((wider, TILE), BF16)] * X,
        me,
        own[0],
        lead,
        *own_parts,
        weight,
        cotangent[0],
        scalars=1,
        flops=2 * TILE * full * full,
    )

    other = col_shift(both, "h", 1)
    own_parts = [col_shift(own_sent[s], "x", s) for s in (1, 2, 3)]
    other, own_parts = join(other, own_parts)
    own = jnp.concatenate([own_sent[0]] + own_parts, axis=1)
    other_sent = call(split_kernel, [((wider, TILE), BF16)] * X, me, other, scalars=1)
    own_core = col_shift(own, "k", 1)
    other_parts = [col_shift(other_sent[s], "x", s) for s in (1, 2, 3)]
    first = jnp.concatenate([own, own_core], axis=1)
    near, far = call(
        first_kernel,
        [((full, 7 * TILE), F32), ((full, 9 * TILE), F32)],
        *forward,
        first,
        flops=2 * 16 * TILE * full * 8 * TILE,
    )
    other_parts, near, far, first = join(other_parts, near, far, first)
    other = jnp.concatenate([other_sent[0]] + other_parts, axis=1)
    source = jnp.concatenate([other, col_shift(other, "k", 1)], axis=1)

    rows = full * full // (X * C) // TILE
    lead1, over1, lead2, over3, lead3, w = call(
        lead_kernel,
        [((full, 3 * TILE), BF16), ((full + rows, TILE), BF16), ((full, TILE), BF16)]
        + [((full + rows, TILE), BF16), ((full, 3 * TILE), BF16), ((rows, TILE), BF16)],
        me,
        forward[1],
        source,
        first,
        far,
        scratch=[pltpu.VMEM((TILE, full), F32)] * 2,
        scalars=1,
        flops=2 * 9 * TILE * full * 8 * TILE,
    )
    near1, near2, near3, run, own, pair = call(
        rest_kernel,
        [((full, TILE), BF16), ((full, TILE), F32), ((full, TILE), BF16)]
        + [((full, 3 * TILE), F32), ((full, TILE), F32), ((rows, TILE), F32)],
        forward[0],
        source,
        near,
        row_shift(lead2, "y", 2),
        w,
        row_shift(w, "z", 2),
        flops=2 * 7 * TILE * full * 8 * TILE,
    )
    parts = join(
        row_shift(lead1, "y", 3),
        row_shift(lead3, "y", 1),
        row_shift(over1, "z", 3),
        row_shift(over3, "z", 1),
    )
    *run, near1, near2, near3, w = call(
        combine_kernel,
        [((full, TILE), BF16)] * 3 + [((full + rows, TILE), BF16)] * 3 + [((rows, TILE), BF16)],
        run,
        near1,
        near2,
        near3,
        pair,
        *parts,
    )
    z_parts = [row_shift(run[s - 1], "z", Z - s) for s in (1, 2, 3)]
    near_parts = [
        row_shift(near, "y", Y - s) for s, near in ((1, near1), (2, near2), (3, near3))
    ]
    z_parts, near_parts = join(z_parts, near_parts)
    w = bf16(sum_of_four([w] + [part[full:] for part in near_parts]))
    (w,) = join(w)
    w_parts = from_x(w)
    back = bf16(total_of(own, [part[:full] for part in near_parts] + z_parts))
    feature_grad = bf16(
        lax.dot_general(
            back, weight, (((0,), (1,)), ((), ())), preferred_element_type=jnp.float32
        )
    )

    parts = jnp.concatenate([w] + w_parts)
    weight_grad = assemble(
        me, parts, col_shift(parts, "k", 1), 1.0 / math.sqrt(nodes_all), full
    )
    return (hidden[None], weight_grad, feature_grad[None])


def solution(mesh):
    in_specs = (
        P("col", "row", None),
        P("row", "col", None, None),
        P("row", "col"),
        P("row", "col", None, None, None),
        P(),
        P("row", "col", None),
    )
    out_specs = (P("row", "col", None), P(), P("col", "row", None))
    return jax.shard_map(body, mesh=mesh, in_specs=in_specs, out_specs=out_specs, check_vma=False)
```

```python
import functools
import math

import jax
import jax.numpy as jnp
from jax import lax
from jax.experimental import pallas as pl
from jax.experimental.pallas import tpu as pltpu
from jax.sharding import PartitionSpec as P

Y = 4
Z = 4
X = 4
H = 2
C = 2
TILE = 128
VMEM_LIMIT = 4 * 1024 * 1024
BF16 = jnp.bfloat16
F32 = jnp.float32


def row_shift(data, axis, step):
    pairs = []
    for r in range(Y * Z):
        y, z = divmod(r, Z)
        if axis == "y":
            source = (y + step) % Y * Z + z
        else:
            source = y * Z + (z + step) % Z
        pairs.append((source, r))
    return lax.ppermute(data, "row", pairs)


def col_shift(data, axis, step):
    pairs = []
    for c in range(X * H * C):
        x, h, k = c // (H * C), c // C % H, c % C
        if axis == "x":
            x = (x + step) % X
        elif axis == "h":
            h = (h + step) % H
        else:
            k = (k + step) % C
        pairs.append(((x * H + h) * C + k, c))
    return lax.ppermute(data, "col", pairs)


def densify_kernel(
    firsts, place_ref, count_ref, values_ref, *refs
):
    *dense_refs, held_ref, sems = refs
    size = dense_refs[0].shape[0]
    part = held_ref.shape[1]
    parts = values_ref.shape[0] // part

    def copy(i):
        return pltpu.make_async_copy(
            values_ref.at[pl.ds(i * part, part)], held_ref.at[i % 2], sems.at[i % 2]
        )

    copy(0).start()

    def clear(i, _):
        rows = pl.ds(pl.multiple_of(i * TILE, TILE), TILE)
        for ref in dense_refs:
            ref[rows, :] = jnp.zeros((TILE, ref.shape[1]), ref.dtype)
        return 0

    lax.fori_loop(0, size // TILE, clear, 0)

    for i in range(parts):
        if i + 1 < parts:
            copy(i + 1).start()
        copy(i).wait()

        def put(k, _):
            r, c = place_ref[0, i * part + k], place_ref[1, i * part + k]
            for first, ref in zip(firsts, dense_refs):

                @pl.when((c >= first) & (c < first + ref.shape[1] // TILE))
                def _():
                    rows = pl.ds(pl.multiple_of(r * TILE, TILE), TILE)
                    columns = pl.ds(pl.multiple_of((c - first) * TILE, TILE), TILE)
                    ref[rows, columns] = held_ref[i % 2, k]

            return 0

        lax.fori_loop(0, jnp.clip(count_ref[0] - i * part, 0, part), put, 0)


def densify(values, place, count, *parts):
    size = 16 * TILE
    vmem = pl.BlockSpec(memory_space=pltpu.VMEM)
    return pl.pallas_call(
        functools.partial(densify_kernel, [first for first, _ in parts]),
        out_shape=[
            jax.ShapeDtypeStruct((size, (last - first) * TILE), values.dtype)
            for first, last in parts
        ],
        in_specs=[
            pl.BlockSpec(memory_space=pltpu.SMEM),
            pl.BlockSpec(memory_space=pltpu.SMEM),
            pl.BlockSpec(memory_space=pltpu.HBM),
        ],
        out_specs=[vmem] * len(parts),
        scratch_shapes=[
            pltpu.VMEM((2, 16, TILE, TILE), values.dtype),
            pltpu.SemaphoreType.DMA((2,)),
        ],
        compiler_params=pltpu.CompilerParams(vmem_limit_bytes=VMEM_LIMIT),
        cost_estimate=pl.CostEstimate(
            flops=0, bytes_accessed=12 * 1024 * 1024, transcendentals=0
        ),
    )(place, count, values)


def products_kernel(pieces, has_added, dense_ref, source_ref, *refs):
    outs = refs[1:] if has_added else refs
    for (first, last, _), out_ref in zip(pieces, outs):
        start = first * TILE
        while start < last * TILE:
            stop = min(start + 4 * TILE, last * TILE)
            total = jnp.dot(
                dense_ref[start:stop, :],
                source_ref[...],
                preferred_element_type=jnp.float32,
            )
            if has_added:
                total += refs[0][start:stop, :]
            out_ref[start - first * TILE : stop - first * TILE, :] = total.astype(out_ref.dtype)
            start = stop


def products(dense, source, added, pieces):
    width = source.shape[1]
    operands = [dense, source] + ([] if added is None else [added])
    vmem = pl.BlockSpec(memory_space=pltpu.VMEM)
    tiles = sum(last - first for first, last, _ in pieces)
    return pl.pallas_call(
        functools.partial(products_kernel, pieces, added is not None),
        out_shape=[
            jax.ShapeDtypeStruct(((last - first) * TILE, width), dtype)
            for first, last, dtype in pieces
        ],
        in_specs=[vmem] * len(operands),
        out_specs=[vmem] * len(pieces),
        compiler_params=pltpu.CompilerParams(vmem_limit_bytes=VMEM_LIMIT),
        cost_estimate=pl.CostEstimate(
            flops=2 * tiles * TILE * width * dense.shape[1],
            bytes_accessed=tiles * TILE * (dense.shape[1] + width) * 4,
            transcendentals=0,
        ),
    )(*operands)


def f32(value):
    return value.astype(jnp.float32)


def bf16(value):
    return value.astype(jnp.bfloat16)


def matmul(a, b):
    return jnp.dot(a, b, preferred_element_type=jnp.float32)


def join(*values):
    return lax.optimization_barrier(values)


def from_z(data):
    return [row_shift(data, "z", s) for s in (1, 2, 3)]


def from_y(data):
    return [row_shift(data, "y", s) for s in (1, 2, 3)]


def from_x(data):
    return [col_shift(data, "x", s) for s in (1, 2, 3)]


def rows_of(data, first, last):
    return data[first * TILE : last * TILE]


def total_of(own, parts):
    total = f32(own)
    for part in parts:
        total += f32(part)
    return total


def cut(value, index, size):
    return lax.dynamic_slice_in_dim(value, index * size, size, 0)


def call(kernel, outs, *operands, scratch=(), scalars=0, flops=0):
    vmem = pl.BlockSpec(memory_space=pltpu.VMEM)
    shapes = [jax.ShapeDtypeStruct(shape, dtype) for shape, dtype in outs]
    return pl.pallas_call(
        kernel,
        out_shape=shapes,
        in_specs=[pl.BlockSpec(memory_space=pltpu.SMEM)] * scalars
        + [vmem] * (len(operands) - scalars),
        out_specs=[vmem] * len(outs),
        scratch_shapes=list(scratch),
        compiler_params=pltpu.CompilerParams(vmem_limit_bytes=VMEM_LIMIT),
        cost_estimate=pl.CostEstimate(
            flops=flops, bytes_accessed=4 * 1024 * 1024, transcendentals=0
        ),
    )(*operands)


def split_for_x(me_x, both_ref, outs):
    full = both_ref.shape[0] // 2
    for s, ref in enumerate(outs):
        first = pl.multiple_of(full + ((me_x - s) & 3) * TILE, TILE)
        ref[:full, :] = both_ref[:full, :]
        ref[full:, :] = both_ref[pl.ds(first, TILE), :]


def middle_kernel(
    me_ref, own_ref, p0, p1, p2, p3, weight_ref, cotangent_ref, hidden_ref, both_ref, *outs
):
    full = weight_ref.shape[0]
    total = own_ref[...] + f32(p0[...]) + f32(p1[...]) + f32(p2[...]) + f32(p3[...])
    summed = bf16(total)
    both_ref[full:, :] = summed.T
    pre = matmul(summed, weight_ref[...])
    sigma = 1.0 / (1.0 + jnp.exp(-pre))
    hidden_ref[...] = bf16(pre * sigma)
    slope = sigma * (1.0 + pre * (1.0 - sigma))
    both_ref[:full, :] = bf16(f32(cotangent_ref[...]) * slope).T
    split_for_x(me_ref[0], both_ref, outs)


def split_kernel(me_ref, both_ref, *outs):
    split_for_x(me_ref[0], both_ref, outs)


def first_kernel(dense1_ref, dense2_ref, source_ref, near_ref, far_ref):
    rows, nodes = near_ref.shape[0], source_ref.shape[1]
    for dense_ref, ref in ((dense1_ref, near_ref), (dense2_ref, far_ref)):
        for first in range(0, ref.shape[1], 4 * TILE):
            span = slice(first, min(first + 4 * TILE, ref.shape[1]))
            ref[:, span] = matmul(source_ref[:rows, :], dense_ref[:nodes, span])


def lead_kernel(me_ref, dense_ref, source_ref, first_ref, added_ref, *refs):
    lead1, over1, lead2, over3, lead3, w_ref, *totals = refs
    full, nodes = lead1.shape[0], source_ref.shape[1]
    for ref, total_ref in zip((first_ref, source_ref), totals):
        total_ref[...] = lax.dot_general(
            ref[full:, :],
            ref[:full, :],
            (((1,), (1,)), ((), ())),
            preferred_element_type=jnp.float32,
        )
    rows = w_ref.shape[0] * TILE // full
    span = pl.ds(pl.multiple_of(me_ref[1] * rows, rows), rows)
    w = bf16(totals[0][span, :] + totals[1][span, :])
    for i in range(full // TILE):
        w_ref[i * rows : (i + 1) * rows, :] = w[:, i * TILE : (i + 1) * TILE]
    for first, last, outs in ((0, 6, (lead1, over1, lead2, over3)), (6, 9, (lead3,))):
        span = slice(first * TILE, last * TILE)
        total = bf16(matmul(source_ref[:full, :], dense_ref[nodes:, span]) + added_ref[:, span])
        start = 0
        for ref in outs:
            ref[:full, :] = total[:, start : start + ref.shape[1]]
            start += ref.shape[1]
    for ref in (over1, over3):
        ref[full:, :] = w_ref[...]


def rest_kernel(dense_ref, source_ref, added_ref, across_ref, w0_ref, w2_ref, *refs):
    near1, near2, near3, run, own, pair = refs
    full, nodes = own.shape[0], source_ref.shape[1]
    pair[...] = f32(w0_ref[...]) + f32(w2_ref[...])
    for first, last, outs in ((0, 4, (own, run)), (4, 7, (near1, near2, near3))):
        span = slice(first * TILE, last * TILE)
        total = matmul(source_ref[:full, :], dense_ref[nodes:, span]) + added_ref[:, span]
        start = 0
        for ref in outs:
            ref[...] = total[:, start : start + ref.shape[1]].astype(ref.dtype)
            start += ref.shape[1]
    run[:, TILE : 2 * TILE] += f32(across_ref[...])


def combine_kernel(
    run, near1, near2, near3, pair, down, up, over1, over3, z1, z2, z3, y1, y2, y3, w_out
):
    full = run.shape[0]
    for s, ref in enumerate((z1, z2, z3)):
        span = slice(s * TILE, (s + 1) * TILE)
        ref[...] = bf16(run[:, span] + f32(down[:, span]) + f32(up[:, span]))
    y1[:full, :] = near1[...]
    y2[:full, :] = bf16(near2[...] + f32(over1[:full, :]) + f32(over3[:full, :]))
    y3[:full, :] = near3[...]
    total = bf16(pair[...] + (f32(over1[full:, :]) + f32(over3[full:, :])))
    for ref in (y1, y2, y3):
        ref[full:, :] = total
    w_out[...] = total


def sum_of_four(parts):
    return (f32(parts[0]) + f32(parts[2])) + (f32(parts[1]) + f32(parts[3]))


def assemble_kernel(me_ref, own_ref, other_ref, out_ref):
    parts = out_ref.shape[1] // TILE
    rows = own_ref.shape[0] // X // parts
    for s in range(X):
        first = (me_ref[0] + s & 3) * C * rows
        for ref, core in ((own_ref, me_ref[1]), (other_ref, 1 - me_ref[1])):
            place = pl.ds(pl.multiple_of(first + core * rows, rows), rows)
            for i in range(parts):
                start = (s * parts + i) * rows
                out_ref[place, i * TILE : (i + 1) * TILE] = ref[start : start + rows, :]


def body(node_features, tile_coords, tile_count, tile_values, weight, cotangent):
    features = node_features[0]
    me_row = lax.axis_index("row")
    me_col = lax.axis_index("col")
    my, mz = me_row >> 2, me_row & 3
    mx, mh, mk = me_col >> 2, me_col >> 1 & 1, me_col & 1
    nodes_all = TILE * Y * Z * X * H * C
    full = features.shape[1]

    tr, tc = tile_coords[0, 0, 0], tile_coords[0, 0, 1]
    place_r = ((tr >> 1) + mh & 1) * 8 + (tr + mk & 1) * 4 + ((tr >> 2) - mx & 3)
    far_y, far_z = (tc >> 2) - my & 3, tc - mz & 3
    place_c = jnp.where(
        far_y == 0, far_z, jnp.where(far_z == 0, 3 + far_y, 3 + far_y * 3 + far_z)
    )
    place = jnp.stack([place_r, place_c])
    values, count = tile_values[0, 0], tile_count[0]

    along_y = from_y(features)
    along_z, along_y[1], forward = join(
        from_z(features), along_y[1], densify(values, place, count, (0, 7), (7, 16))
    )
    rest = jnp.concatenate(along_z)
    near = jnp.concatenate([features, rest] + along_y)
    far = [row_shift(rest, "y", 1), row_shift(rest, "y", 3)]
    far += [row_shift(along_y[1], "z", 1), row_shift(along_y[1], "z", 3)]
    far += [row_shift(along_z[1], "y", 2)]
    far, near = join(far, products(forward[0], near, None, [(0, 16, F32)])[0])
    far = jnp.concatenate([far[0], far[2], far[4], far[3], far[1]])

    (away,) = products(forward[1], far, near, [(12, 16, BF16)])
    away, far = join(away, far)
    arrived = col_shift(away, "k", 1)
    home, away, own = products(
        forward[1], far, near, [(8, 12, F32), (4, 8, BF16), (0, 4, F32)]
    )
    home, arrived, away, own = join(home, arrived, away, own)
    lead = [bf16(rows_of(home, s, s + 1) + f32(rows_of(arrived, s, s + 1))) for s in range(X)]
    lead_parts = [col_shift(lead[s], "x", X - s) for s in (1, 2, 3)]
    lead, arrived = lead[0], col_shift(away, "k", 1)
    lead = bf16(total_of(lead, lead_parts))
    own = [rows_of(own, s, s + 1) + f32(rows_of(arrived, s, s + 1)) for s in range(X)]
    lead = col_shift(lead, "h", 1)
    own_parts = [col_shift(bf16(own[s]), "x", X - s) for s in (1, 2, 3)]
    me = jnp.stack([mx, mk])
    wider = full + TILE
    hidden, both, *own_sent = call(
        middle_kernel,
        [((TILE, full), BF16), ((2 * full, TILE), BF16)] + [((wider, TILE), BF16)] * X,
        me,
        own[0],
        lead,
        *own_parts,
        weight,
        cotangent[0],
        scalars=1,
        flops=2 * TILE * full * full,
    )

    other = col_shift(both, "h", 1)
    own_parts = [col_shift(own_sent[s], "x", s) for s in (1, 2, 3)]
    other, own_parts = join(other, own_parts)
    own = jnp.concatenate([own_sent[0]] + own_parts, axis=1)
    other_sent = call(split_kernel, [((wider, TILE), BF16)] * X, me, other, scalars=1)
    own_core = col_shift(own, "k", 1)
    other_parts = [col_shift(other_sent[s], "x", s) for s in (1, 2, 3)]
    first = jnp.concatenate([own, own_core], axis=1)
    near, far = call(
        first_kernel,
        [((full, 7 * TILE), F32), ((full, 9 * TILE), F32)],
        *forward,
        first,
        flops=2 * 16 * TILE * full * 8 * TILE,
    )
    other_parts, near, far, first = join(other_parts, near, far, first)
    other = jnp.concatenate([other_sent[0]] + other_parts, axis=1)
    source = jnp.concatenate([other, col_shift(other, "k", 1)], axis=1)

    rows = full * full // (X * C) // TILE
    lead1, over1, lead2, over3, lead3, w = call(
        lead_kernel,
        [((full, 3 * TILE), BF16), ((full + rows, TILE), BF16), ((full, TILE), BF16)]
        + [((full + rows, TILE), BF16), ((full, 3 * TILE), BF16), ((rows, TILE), BF16)],
        me,
        forward[1],
        source,
        first,
        far,
        scratch=[pltpu.VMEM((TILE, full), F32)] * 2,
        scalars=1,
        flops=2 * 9 * TILE * full * 8 * TILE,
    )
    near1, near2, near3, run, own, pair = call(
        rest_kernel,
        [((full, TILE), BF16), ((full, TILE), F32), ((full, TILE), BF16)]
        + [((full, 3 * TILE), F32), ((full, TILE), F32), ((rows, TILE), F32)],
        forward[0],
        source,
        near,
        row_shift(lead2, "y", 2),
        w,
        row_shift(w, "z", 2),
        flops=2 * 7 * TILE * full * 8 * TILE,
    )
    parts = join(
        row_shift(lead1, "y", 3),
        row_shift(lead3, "y", 1),
        row_shift(over1, "z", 3),
        row_shift(over3, "z", 1),
    )
    *run, near1, near2, near3, w = call(
        combine_kernel,
        [((full, TILE), BF16)] * 3 + [((full + rows, TILE), BF16)] * 3 + [((rows, TILE), BF16)],
        run,
        near1,
        near2,
        near3,
        pair,
        *parts,
    )
    z_parts = [row_shift(run[s - 1], "z", Z - s) for s in (1, 2, 3)]
    near_parts = [
        row_shift(near, "y", Y - s) for s, near in ((1, near1), (2, near2), (3, near3))
    ]
    z_parts, near_parts = join(z_parts, near_parts)
    w = bf16(sum_of_four([w] + [part[full:] for part in near_parts]))
    (w,) = join(w)
    w_parts = from_x(w)
    back = bf16(total_of(own, [part[:full] for part in near_parts] + z_parts))
    feature_grad = bf16(
        lax.dot_general(
            back, weight, (((0,), (1,)), ((), ())), preferred_element_type=jnp.float32
        )
    )

    parts = jnp.concatenate([w] + w_parts)
    (w,) = call(
        assemble_kernel, [((full, full), BF16)], me, parts, col_shift(parts, "k", 1), scalars=1
    )
    weight_grad = f32(w) / math.sqrt(nodes_all)
    return (hidden[None], weight_grad, feature_grad[None])


def solution(mesh):
    in_specs = (
        P("col", "row", None),
        P("row", "col", None, None),
        P("row", "col"),
        P("row", "col", None, None, None),
        P(),
        P("row", "col", None),
    )
    out_specs = (P("row", "col", None), P(), P("col", "row", None))
    return jax.shard_map(body, mesh=mesh, in_specs=in_specs, out_specs=out_specs, check_vma=False)
```

```python
import functools
import math

import jax
import jax.numpy as jnp
from jax import lax
from jax.experimental import pallas as pl
from jax.experimental.pallas import tpu as pltpu
from jax.sharding import PartitionSpec as P

Y = 4
Z = 4
X = 4
H = 2
C = 2
TILE = 128
VMEM_LIMIT = 4 * 1024 * 1024
STEP = 256
BF16 = jnp.bfloat16
F32 = jnp.float32


def row_shift(data, axis, step):
    pairs = []
    for r in range(Y * Z):
        y, z = divmod(r, Z)
        if axis == "y":
            source = (y + step) % Y * Z + z
        else:
            source = y * Z + (z + step) % Z
        pairs.append((source, r))
    return lax.ppermute(data, "row", pairs)


def col_shift(data, axis, step):
    pairs = []
    for c in range(X * H * C):
        x, h, k = c // (H * C), c // C % H, c % C
        if axis == "x":
            x = (x + step) % X
        elif axis == "h":
            h = (h + step) % H
        else:
            k = (k + step) % C
        pairs.append(((x * H + h) * C + k, c))
    return lax.ppermute(data, "col", pairs)


def densify_kernel(
    firsts, place_ref, count_ref, values_ref, *refs
):
    *dense_refs, held_ref, sems = refs
    size = dense_refs[0].shape[0]
    part = held_ref.shape[1]
    parts = values_ref.shape[0] // part

    def copy(i):
        return pltpu.make_async_copy(
            values_ref.at[pl.ds(i * part, part)], held_ref.at[i & 1], sems.at[i & 1]
        )

    copy(0).start()

    def clear(i, _):
        rows = pl.ds(pl.multiple_of(i * TILE, TILE), TILE)
        for ref in dense_refs:
            ref[rows, :] = jnp.zeros((TILE, ref.shape[1]), ref.dtype)
        return 0

    lax.fori_loop(0, size // TILE, clear, 0)

    def place_part(i, _):
        @pl.when(i + 1 < parts)
        def _():
            copy(i + 1).start()

        copy(i).wait()

        def put(k, _):
            r, c = place_ref[0, i * part + k], place_ref[1, i * part + k]
            for first, ref in zip(firsts, dense_refs):

                @pl.when((c >= first) & (c < first + ref.shape[1] // TILE))
                def _():
                    rows = pl.ds(pl.multiple_of(r * TILE, TILE), TILE)
                    columns = pl.ds(pl.multiple_of((c - first) * TILE, TILE), TILE)
                    ref[rows, columns] = held_ref[i & 1, k]

            return 0

        lax.fori_loop(0, jnp.clip(count_ref[0] - i * part, 0, part), put, 0)
        return 0

    lax.fori_loop(0, parts, place_part, 0)


def densify(values, place, count, *parts):
    size = 16 * TILE
    vmem = pl.BlockSpec(memory_space=pltpu.VMEM)
    return pl.pallas_call(
        functools.partial(densify_kernel, [first for first, _ in parts]),
        out_shape=[
            jax.ShapeDtypeStruct((size, (last - first) * TILE), values.dtype)
            for first, last in parts
        ],
        in_specs=[
            pl.BlockSpec(memory_space=pltpu.SMEM),
            pl.BlockSpec(memory_space=pltpu.SMEM),
            pl.BlockSpec(memory_space=pltpu.HBM),
        ],
        out_specs=[vmem] * len(parts),
        scratch_shapes=[
            pltpu.VMEM((2, 16, TILE, TILE), values.dtype),
            pltpu.SemaphoreType.DMA((2,)),
        ],
        compiler_params=pltpu.CompilerParams(vmem_limit_bytes=VMEM_LIMIT),
        cost_estimate=pl.CostEstimate(
            flops=0, bytes_accessed=12 * 1024 * 1024, transcendentals=0
        ),
    )(place, count, values)


def products_kernel(size, pieces, has_added, dense_ref, source_ref, *refs):
    outs = refs[1:] if has_added else refs
    for (first, last, _), out_ref in zip(pieces, outs):

        def step(i, _):
            start = pl.multiple_of(i * size, size)
            span = pl.ds(first * TILE + start, size)
            total = jnp.dot(
                dense_ref[span, :], source_ref[...], preferred_element_type=jnp.float32
            )
            if has_added:
                total += refs[0][span, :]
            out_ref[pl.ds(start, size), :] = total.astype(out_ref.dtype)
            return 0

        lax.fori_loop(0, (last - first) * TILE // size, step, 0)


def products(dense, source, added, size, pieces):
    width = source.shape[1]
    operands = [dense, source] + ([] if added is None else [added])
    vmem = pl.BlockSpec(memory_space=pltpu.VMEM)
    tiles = sum(last - first for first, last, _ in pieces)
    return pl.pallas_call(
        functools.partial(products_kernel, size, pieces, added is not None),
        out_shape=[
            jax.ShapeDtypeStruct(((last - first) * TILE, width), dtype)
            for first, last, dtype in pieces
        ],
        in_specs=[vmem] * len(operands),
        out_specs=[vmem] * len(pieces),
        compiler_params=pltpu.CompilerParams(vmem_limit_bytes=VMEM_LIMIT),
        cost_estimate=pl.CostEstimate(
            flops=2 * tiles * TILE * width * dense.shape[1],
            bytes_accessed=tiles * TILE * (dense.shape[1] + width) * 4,
            transcendentals=0,
        ),
    )(*operands)


def f32(value):
    return value.astype(jnp.float32)


def bf16(value):
    return value.astype(jnp.bfloat16)


def matmul(a, b):
    return jnp.dot(a, b, preferred_element_type=jnp.float32)


def join(*values):
    return lax.optimization_barrier(values)


def from_z(data):
    return [row_shift(data, "z", s) for s in (1, 2, 3)]


def from_y(data):
    return [row_shift(data, "y", s) for s in (1, 2, 3)]


def from_x(data):
    return [col_shift(data, "x", s) for s in (1, 2, 3)]


def rows_of(data, first, last):
    return data[first * TILE : last * TILE]


def total_of(own, parts):
    total = f32(own)
    for part in parts:
        total += f32(part)
    return total


def cut(value, index, size):
    return lax.dynamic_slice_in_dim(value, index * size, size, 0)


def call(kernel, outs, *operands, scratch=(), scalars=0, flops=0):
    vmem = pl.BlockSpec(memory_space=pltpu.VMEM)
    shapes = [jax.ShapeDtypeStruct(shape, dtype) for shape, dtype in outs]
    return pl.pallas_call(
        kernel,
        out_shape=shapes,
        in_specs=[pl.BlockSpec(memory_space=pltpu.SMEM)] * scalars
        + [vmem] * (len(operands) - scalars),
        out_specs=[vmem] * len(outs),
        scratch_shapes=list(scratch),
        compiler_params=pltpu.CompilerParams(vmem_limit_bytes=VMEM_LIMIT),
        cost_estimate=pl.CostEstimate(
            flops=flops, bytes_accessed=4 * 1024 * 1024, transcendentals=0
        ),
    )(*operands)


def split_for_x(me_x, both_ref, outs):
    full = both_ref.shape[0] // 2
    for s, ref in enumerate(outs):
        first = pl.multiple_of(full + ((me_x - s) & 3) * TILE, TILE)
        ref[:full, :] = both_ref[:full, :]
        ref[full:, :] = both_ref[pl.ds(first, TILE), :]


def middle_kernel(
    me_ref, own_ref, p0, p1, p2, p3, weight_ref, cotangent_ref, hidden_ref, both_ref, *outs
):
    full = weight_ref.shape[0]
    total = own_ref[...] + f32(p0[...]) + f32(p1[...]) + f32(p2[...]) + f32(p3[...])
    summed = bf16(total)
    both_ref[full:, :] = summed.T
    pre = matmul(summed, weight_ref[...])
    sigma = 1.0 / (1.0 + jnp.exp(-pre))
    hidden_ref[...] = bf16(pre * sigma)
    slope = sigma * (1.0 + pre * (1.0 - sigma))
    both_ref[:full, :] = bf16(f32(cotangent_ref[...]) * slope).T
    split_for_x(me_ref[0], both_ref, outs)


def split_kernel(me_ref, both_ref, *outs):
    split_for_x(me_ref[0], both_ref, outs)


def first_kernel(dense1_ref, dense2_ref, source_ref, near_ref, far_ref):
    nodes = source_ref.shape[1]
    for dense_ref, ref in ((dense1_ref, near_ref), (dense2_ref, far_ref)):

        def step(i, _):
            here = pl.ds(pl.multiple_of(i * TILE, TILE), TILE)
            ref[here, :] = matmul(source_ref[here, :], dense_ref[:nodes, :])
            return 0

        lax.fori_loop(0, ref.shape[0] // TILE, step, 0)


def lead_kernel(me_ref, dense_ref, source_ref, first_ref, added_ref, *refs):
    lead1, over1, lead2, over3, lead3, w_ref, *totals = refs
    full, nodes = lead1.shape[0], source_ref.shape[1]
    for ref, total_ref in zip((first_ref, source_ref), totals):

        def step(i, _):
            here = pl.ds(pl.multiple_of(i * TILE, TILE), TILE)
            total_ref[:, here] = lax.dot_general(
                ref[full:, :],
                ref[here, :],
                (((1,), (1,)), ((), ())),
                preferred_element_type=jnp.float32,
            )
            return 0

        lax.fori_loop(0, full // TILE, step, 0)
    rows = w_ref.shape[0] * TILE // full
    span = pl.ds(pl.multiple_of(me_ref[1] * rows, rows), rows)
    w = bf16(totals[0][span, :] + totals[1][span, :])
    for i in range(full // TILE):
        w_ref[i * rows : (i + 1) * rows, :] = w[:, i * TILE : (i + 1) * TILE]

    def step(i, _):
        here = pl.ds(pl.multiple_of(i * STEP, STEP), STEP)
        total = bf16(matmul(source_ref[here, :], dense_ref[nodes:, :]) + added_ref[here, :])
        start = 0
        for ref in (lead1, over1, lead2, over3, lead3):
            ref[here, :] = total[:, start : start + ref.shape[1]]
            start += ref.shape[1]
        return 0

    lax.fori_loop(0, full // STEP, step, 0)
    for ref in (over1, over3):
        ref[full:, :] = w_ref[...]


def rest_kernel(dense_ref, source_ref, added_ref, across_ref, w0_ref, w2_ref, *refs):
    near1, near2, near3, run, own, pair = refs
    full, nodes = own.shape[0], source_ref.shape[1]
    pair[...] = f32(w0_ref[...]) + f32(w2_ref[...])

    def step(i, _):
        here = pl.ds(pl.multiple_of(i * STEP, STEP), STEP)
        total = matmul(source_ref[here, :], dense_ref[nodes:, :]) + added_ref[here, :]
        start = 0
        for ref in (own, run, near1, near2, near3):
            ref[here, :] = total[:, start : start + ref.shape[1]].astype(ref.dtype)
            start += ref.shape[1]
        return 0

    lax.fori_loop(0, full // STEP, step, 0)
    run[:, TILE : 2 * TILE] += f32(across_ref[...])


def combine_kernel(
    run, near1, near2, near3, pair, down, up, over1, over3, z1, z2, z3, y1, y2, y3, w_out
):
    full = run.shape[0]
    for s, ref in enumerate((z1, z2, z3)):
        span = slice(s * TILE, (s + 1) * TILE)
        ref[...] = bf16(run[:, span] + f32(down[:, span]) + f32(up[:, span]))
    y1[:full, :] = near1[...]
    y2[:full, :] = bf16(near2[...] + f32(over1[:full, :]) + f32(over3[:full, :]))
    y3[:full, :] = near3[...]
    total = bf16(pair[...] + (f32(over1[full:, :]) + f32(over3[full:, :])))
    for ref in (y1, y2, y3):
        ref[full:, :] = total
    w_out[...] = total


def sum_of_four(parts):
    return (f32(parts[0]) + f32(parts[2])) + (f32(parts[1]) + f32(parts[3]))


def assemble_kernel(me_ref, own_ref, other_ref, out_ref):
    parts = out_ref.shape[1] // TILE
    rows = own_ref.shape[0] // X // parts
    for s in range(X):
        first = (me_ref[0] + s & 3) * C * rows
        for ref, core in ((own_ref, me_ref[1]), (other_ref, 1 - me_ref[1])):
            place = pl.ds(pl.multiple_of(first + core * rows, rows), rows)
            for i in range(parts):
                start = (s * parts + i) * rows
                out_ref[place, i * TILE : (i + 1) * TILE] = ref[start : start + rows, :]


def body(node_features, tile_coords, tile_count, tile_values, weight, cotangent):
    features = node_features[0]
    me_row = lax.axis_index("row")
    me_col = lax.axis_index("col")
    my, mz = me_row >> 2, me_row & 3
    mx, mh, mk = me_col >> 2, me_col >> 1 & 1, me_col & 1
    nodes_all = TILE * Y * Z * X * H * C
    full = features.shape[1]

    tr, tc = tile_coords[0, 0, 0], tile_coords[0, 0, 1]
    place_r = ((tr >> 1) + mh & 1) * 8 + (tr + mk & 1) * 4 + ((tr >> 2) - mx & 3)
    far_y, far_z = (tc >> 2) - my & 3, tc - mz & 3
    place_c = jnp.where(
        far_y == 0, far_z, jnp.where(far_z == 0, 3 + far_y, 3 + far_y * 3 + far_z)
    )
    place = jnp.stack([place_r, place_c])
    values, count = tile_values[0, 0], tile_count[0]

    along_y = from_y(features)
    along_z, along_y[1], forward = join(
        from_z(features), along_y[1], densify(values, place, count, (0, 7), (7, 16))
    )
    rest = jnp.concatenate(along_z)
    near = jnp.concatenate([features, rest] + along_y)
    far = [row_shift(rest, "y", 1), row_shift(rest, "y", 3)]
    far += [row_shift(along_y[1], "z", 1), row_shift(along_y[1], "z", 3)]
    far += [row_shift(along_z[1], "y", 2)]
    far, near = join(far, products(forward[0], near, None, TILE, [(0, 16, F32)])[0])
    far = jnp.concatenate([far[0], far[2], far[4], far[3], far[1]])

    (away,) = products(forward[1], far, near, 512, [(12, 16, BF16)])
    away, far = join(away, far)
    arrived = col_shift(away, "k", 1)
    (rest,) = products(forward[1], far, near, 512, [(0, 12, F32)])
    home, away, own = rows_of(rest, 8, 12), bf16(rows_of(rest, 4, 8)), rows_of(rest, 0, 4)
    home, arrived, away, own = join(home, arrived, away, own)
    lead = [bf16(rows_of(home, s, s + 1) + f32(rows_of(arrived, s, s + 1))) for s in range(X)]
    lead_parts = [col_shift(lead[s], "x", X - s) for s in (1, 2, 3)]
    lead, arrived = lead[0], col_shift(away, "k", 1)
    lead = bf16(total_of(lead, lead_parts))
    own = [rows_of(own, s, s + 1) + f32(rows_of(arrived, s, s + 1)) for s in range(X)]
    lead = col_shift(lead, "h", 1)
    own_parts = [col_shift(bf16(own[s]), "x", X - s) for s in (1, 2, 3)]
    me = jnp.stack([mx, mk])
    wider = full + TILE
    hidden, both, *own_sent = call(
        middle_kernel,
        [((TILE, full), BF16), ((2 * full, TILE), BF16)] + [((wider, TILE), BF16)] * X,
        me,
        own[0],
        lead,
        *own_parts,
        weight,
        cotangent[0],
        scalars=1,
        flops=2 * TILE * full * full,
    )

    other = col_shift(both, "h", 1)
    own_parts = [col_shift(own_sent[s], "x", s) for s in (1, 2, 3)]
    other, own_parts = join(other, own_parts)
    own = jnp.concatenate([own_sent[0]] + own_parts, axis=1)
    other_sent = call(split_kernel, [((wider, TILE), BF16)] * X, me, other, scalars=1)
    own_core = col_shift(own, "k", 1)
    other_parts = [col_shift(other_sent[s], "x", s) for s in (1, 2, 3)]
    first = jnp.concatenate([own, own_core], axis=1)
    near, far = call(
        first_kernel,
        [((full, 7 * TILE), F32), ((full, 9 * TILE), F32)],
        *forward,
        first,
        flops=2 * 16 * TILE * full * 8 * TILE,
    )
    other_parts, near, far, first = join(other_parts, near, far, first)
    other = jnp.concatenate([other_sent[0]] + other_parts, axis=1)
    source = jnp.concatenate([other, col_shift(other, "k", 1)], axis=1)

    rows = full * full // (X * C) // TILE
    lead1, over1, lead2, over3, lead3, w = call(
        lead_kernel,
        [((full, 3 * TILE), BF16), ((full + rows, TILE), BF16), ((full, TILE), BF16)]
        + [((full + rows, TILE), BF16), ((full, 3 * TILE), BF16), ((rows, TILE), BF16)],
        me,
        forward[1],
        source,
        first,
        far,
        scratch=[pltpu.VMEM((TILE, full), F32)] * 2,
        scalars=1,
        flops=2 * 9 * TILE * full * 8 * TILE,
    )
    near1, near2, near3, run, own, pair = call(
        rest_kernel,
        [((full, TILE), BF16), ((full, TILE), F32), ((full, TILE), BF16)]
        + [((full, 3 * TILE), F32), ((full, TILE), F32), ((rows, TILE), F32)],
        forward[0],
        source,
        near,
        row_shift(lead2, "y", 2),
        w,
        row_shift(w, "z", 2),
        flops=2 * 7 * TILE * full * 8 * TILE,
    )
    parts = join(
        row_shift(lead1, "y", 3),
        row_shift(lead3, "y", 1),
        row_shift(over1, "z", 3),
        row_shift(over3, "z", 1),
    )
    *run, near1, near2, near3, w = call(
        combine_kernel,
        [((full, TILE), BF16)] * 3 + [((full + rows, TILE), BF16)] * 3 + [((rows, TILE), BF16)],
        run,
        near1,
        near2,
        near3,
        pair,
        *parts,
    )
    z_parts = [row_shift(run[s - 1], "z", Z - s) for s in (1, 2, 3)]
    near_parts = [
        row_shift(near, "y", Y - s) for s, near in ((1, near1), (2, near2), (3, near3))
    ]
    z_parts, near_parts = join(z_parts, near_parts)
    w = bf16(sum_of_four([w] + [part[full:] for part in near_parts]))
    (w,) = join(w)
    w_parts = from_x(w)
    back = bf16(total_of(own, [part[:full] for part in near_parts] + z_parts))
    feature_grad = bf16(
        lax.dot_general(
            back, weight, (((0,), (1,)), ((), ())), preferred_element_type=jnp.float32
        )
    )

    parts = jnp.concatenate([w] + w_parts)
    (w,) = call(
        assemble_kernel, [((full, full), BF16)], me, parts, col_shift(parts, "k", 1), scalars=1
    )
    weight_grad = f32(w) / math.sqrt(nodes_all)
    return (hidden[None], weight_grad, feature_grad[None])


def solution(mesh):
    in_specs = (
        P("col", "row", None),
        P("row", "col", None, None),
        P("row", "col"),
        P("row", "col", None, None, None),
        P(),
        P("row", "col", None),
    )
    out_specs = (P("row", "col", None), P(), P("col", "row", None))
    return jax.shard_map(body, mesh=mesh, in_specs=in_specs, out_specs=out_specs, check_vma=False)
```

```python
import functools
import math

import jax
import jax.numpy as jnp
from jax import lax
from jax.experimental import pallas as pl
from jax.experimental.pallas import tpu as pltpu
from jax.sharding import PartitionSpec as P

Y = 4
Z = 4
X = 4
H = 2
C = 2
TILE = 128
VMEM_LIMIT = 4 * 1024 * 1024
STEP = 256
BF16 = jnp.bfloat16
F32 = jnp.float32


def row_shift(data, axis, step):
    pairs = []
    for r in range(Y * Z):
        y, z = divmod(r, Z)
        if axis == "y":
            source = (y + step) % Y * Z + z
        else:
            source = y * Z + (z + step) % Z
        pairs.append((source, r))
    return lax.ppermute(data, "row", pairs)


def col_shift(data, axis, step):
    pairs = []
    for c in range(X * H * C):
        x, h, k = c // (H * C), c // C % H, c % C
        if axis == "x":
            x = (x + step) % X
        elif axis == "h":
            h = (h + step) % H
        else:
            k = (k + step) % C
        pairs.append(((x * H + h) * C + k, c))
    return lax.ppermute(data, "col", pairs)


def densify_kernel(
    firsts, place_ref, count_ref, values_ref, *refs
):
    *dense_refs, held_ref, sems = refs
    size = dense_refs[0].shape[0]
    part = held_ref.shape[1]
    parts = values_ref.shape[0] // part

    def copy(i):
        return pltpu.make_async_copy(
            values_ref.at[pl.ds(i * part, part)], held_ref.at[i & 1], sems.at[i & 1]
        )

    copy(0).start()

    def clear(i, _):
        rows = pl.ds(pl.multiple_of(i * TILE, TILE), TILE)
        for ref in dense_refs:
            ref[rows, :] = jnp.zeros((TILE, ref.shape[1]), ref.dtype)
        return 0

    lax.fori_loop(0, size // TILE, clear, 0)

    def place_part(i, _):
        @pl.when(i + 1 < parts)
        def _():
            copy(i + 1).start()

        copy(i).wait()

        def put(k, _):
            r, c = place_ref[0, i * part + k], place_ref[1, i * part + k]
            for first, ref in zip(firsts, dense_refs):

                @pl.when((c >= first) & (c < first + ref.shape[1] // TILE))
                def _():
                    rows = pl.ds(pl.multiple_of(r * TILE, TILE), TILE)
                    columns = pl.ds(pl.multiple_of((c - first) * TILE, TILE), TILE)
                    ref[rows, columns] = held_ref[i & 1, k]

            return 0

        lax.fori_loop(0, jnp.clip(count_ref[0] - i * part, 0, part), put, 0)
        return 0

    lax.fori_loop(0, parts, place_part, 0)


def densify(values, place, count, *parts):
    size = 16 * TILE
    vmem = pl.BlockSpec(memory_space=pltpu.VMEM)
    return pl.pallas_call(
        functools.partial(densify_kernel, [first for first, _ in parts]),
        out_shape=[
            jax.ShapeDtypeStruct((size, (last - first) * TILE), values.dtype)
            for first, last in parts
        ],
        in_specs=[
            pl.BlockSpec(memory_space=pltpu.SMEM),
            pl.BlockSpec(memory_space=pltpu.SMEM),
            pl.BlockSpec(memory_space=pltpu.HBM),
        ],
        out_specs=[vmem] * len(parts),
        scratch_shapes=[
            pltpu.VMEM((2, 16, TILE, TILE), values.dtype),
            pltpu.SemaphoreType.DMA((2,)),
        ],
        compiler_params=pltpu.CompilerParams(vmem_limit_bytes=VMEM_LIMIT),
        cost_estimate=pl.CostEstimate(
            flops=0, bytes_accessed=12 * 1024 * 1024, transcendentals=0
        ),
    )(place, count, values)


def products_kernel(size, pieces, has_added, dense_ref, source_ref, *refs):
    outs = refs[1:] if has_added else refs
    for (first, last, _), out_ref in zip(pieces, outs):

        def step(i, _):
            start = pl.multiple_of(i * size, size)
            span = pl.ds(first * TILE + start, size)
            total = jnp.dot(
                dense_ref[span, :], source_ref[...], preferred_element_type=jnp.float32
            )
            if has_added:
                total += refs[0][span, :]
            out_ref[pl.ds(start, size), :] = total.astype(out_ref.dtype)
            return 0

        lax.fori_loop(0, (last - first) * TILE // size, step, 0)


def products(dense, source, added, size, pieces):
    width = source.shape[1]
    operands = [dense, source] + ([] if added is None else [added])
    vmem = pl.BlockSpec(memory_space=pltpu.VMEM)
    tiles = sum(last - first for first, last, _ in pieces)
    return pl.pallas_call(
        functools.partial(products_kernel, size, pieces, added is not None),
        out_shape=[
            jax.ShapeDtypeStruct(((last - first) * TILE, width), dtype)
            for first, last, dtype in pieces
        ],
        in_specs=[vmem] * len(operands),
        out_specs=[vmem] * len(pieces),
        compiler_params=pltpu.CompilerParams(vmem_limit_bytes=VMEM_LIMIT),
        cost_estimate=pl.CostEstimate(
            flops=2 * tiles * TILE * width * dense.shape[1],
            bytes_accessed=tiles * TILE * (dense.shape[1] + width) * 4,
            transcendentals=0,
        ),
    )(*operands)


def f32(value):
    return value.astype(jnp.float32)


def bf16(value):
    return value.astype(jnp.bfloat16)


def matmul(a, b):
    return jnp.dot(a, b, preferred_element_type=jnp.float32)


def join(*values):
    return lax.optimization_barrier(values)


def from_z(data):
    return [row_shift(data, "z", s) for s in (1, 2, 3)]


def from_y(data):
    return [row_shift(data, "y", s) for s in (1, 2, 3)]


def from_x(data):
    return [col_shift(data, "x", s) for s in (1, 2, 3)]


def rows_of(data, first, last):
    return data[first * TILE : last * TILE]


def total_of(own, parts):
    total = f32(own)
    for part in parts:
        total += f32(part)
    return total


def cut(value, index, size):
    return lax.dynamic_slice_in_dim(value, index * size, size, 0)


def call(kernel, outs, *operands, scratch=(), scalars=0, flops=0):
    vmem = pl.BlockSpec(memory_space=pltpu.VMEM)
    shapes = [jax.ShapeDtypeStruct(shape, dtype) for shape, dtype in outs]
    return pl.pallas_call(
        kernel,
        out_shape=shapes,
        in_specs=[pl.BlockSpec(memory_space=pltpu.SMEM)] * scalars
        + [vmem] * (len(operands) - scalars),
        out_specs=[vmem] * len(outs),
        scratch_shapes=list(scratch),
        compiler_params=pltpu.CompilerParams(vmem_limit_bytes=VMEM_LIMIT),
        cost_estimate=pl.CostEstimate(
            flops=flops, bytes_accessed=4 * 1024 * 1024, transcendentals=0
        ),
    )(*operands)


def split_for_x(me_x, both_ref, outs):
    full = both_ref.shape[0] // 2
    for s, ref in enumerate(outs):
        first = pl.multiple_of(full + ((me_x - s) & 3) * TILE, TILE)
        ref[:full, :] = both_ref[:full, :]
        ref[full:, :] = both_ref[pl.ds(first, TILE), :]


def middle_kernel(
    me_ref, own_ref, p0, p1, p2, p3, weight_ref, cotangent_ref, hidden_ref, both_ref, *outs
):
    full = weight_ref.shape[0]
    total = own_ref[...] + f32(p0[...]) + f32(p1[...]) + f32(p2[...]) + f32(p3[...])
    summed = bf16(total)
    both_ref[full:, :] = summed.T
    pre = matmul(summed, weight_ref[...])
    sigma = 1.0 / (1.0 + jnp.exp(-pre))
    hidden_ref[...] = bf16(pre * sigma)
    slope = sigma * (1.0 + pre * (1.0 - sigma))
    both_ref[:full, :] = bf16(f32(cotangent_ref[...]) * slope).T
    split_for_x(me_ref[0], both_ref, outs)


def split_kernel(me_ref, both_ref, *outs):
    split_for_x(me_ref[0], both_ref, outs)


def weight_rows(source_ref, total_ref):
    full = total_ref.shape[1]

    def step(i, _):
        here = pl.ds(pl.multiple_of(i * STEP, STEP), STEP)
        total_ref[:, here] = lax.dot_general(
            source_ref[full:, :],
            source_ref[here, :],
            (((1,), (1,)), ((), ())),
            preferred_element_type=jnp.float32,
        )
        return 0

    lax.fori_loop(0, full // STEP, step, 0)


def first_kernel(dense1_ref, dense2_ref, source_ref, near_ref, far_ref, total_ref):
    nodes = source_ref.shape[1]
    weight_rows(source_ref, total_ref)
    for dense_ref, ref in ((dense1_ref, near_ref), (dense2_ref, far_ref)):

        def step(i, _):
            here = pl.ds(pl.multiple_of(i * TILE, TILE), TILE)
            ref[here, :] = matmul(source_ref[here, :], dense_ref[:nodes, :])
            return 0

        lax.fori_loop(0, ref.shape[0] // TILE, step, 0)


def lead_kernel(me_ref, dense_ref, source_ref, first_ref, added_ref, *refs):
    lead1, over1, lead2, over3, lead3, w_ref, total_ref = refs
    full, nodes = lead1.shape[0], source_ref.shape[1]
    weight_rows(source_ref, total_ref)
    rows = w_ref.shape[0] * TILE // full
    span = pl.ds(pl.multiple_of(me_ref[1] * rows, rows), rows)
    w = bf16(first_ref[span, :] + total_ref[span, :])
    for i in range(full // TILE):
        w_ref[i * rows : (i + 1) * rows, :] = w[:, i * TILE : (i + 1) * TILE]

    def step(i, _):
        here = pl.ds(pl.multiple_of(i * STEP, STEP), STEP)
        total = bf16(matmul(source_ref[here, :], dense_ref[nodes:, :]) + added_ref[here, :])
        start = 0
        for ref in (lead1, over1, lead2, over3, lead3):
            ref[here, :] = total[:, start : start + ref.shape[1]]
            start += ref.shape[1]
        return 0

    lax.fori_loop(0, full // STEP, step, 0)
    for ref in (over1, over3):
        ref[full:, :] = w_ref[...]


def rest_kernel(dense_ref, source_ref, added_ref, across_ref, w0_ref, w2_ref, *refs):
    near1, near2, near3, run, own, pair = refs
    full, nodes = own.shape[0], source_ref.shape[1]
    pair[...] = f32(w0_ref[...]) + f32(w2_ref[...])

    def step(i, _):
        here = pl.ds(pl.multiple_of(i * STEP, STEP), STEP)
        total = matmul(source_ref[here, :], dense_ref[nodes:, :]) + added_ref[here, :]
        start = 0
        for ref in (own, run, near1, near2, near3):
            ref[here, :] = total[:, start : start + ref.shape[1]].astype(ref.dtype)
            start += ref.shape[1]
        return 0

    lax.fori_loop(0, full // STEP, step, 0)
    run[:, TILE : 2 * TILE] += f32(across_ref[...])


def combine_kernel(
    run, near1, near2, near3, pair, down, up, over1, over3, z1, z2, z3, y1, y2, y3, w_out
):
    full = run.shape[0]
    for s, ref in enumerate((z1, z2, z3)):
        span = slice(s * TILE, (s + 1) * TILE)
        ref[...] = bf16(run[:, span] + f32(down[:, span]) + f32(up[:, span]))
    y1[:full, :] = near1[...]
    y2[:full, :] = bf16(near2[...] + f32(over1[:full, :]) + f32(over3[:full, :]))
    y3[:full, :] = near3[...]
    total = bf16(pair[...] + (f32(over1[full:, :]) + f32(over3[full:, :])))
    for ref in (y1, y2, y3):
        ref[full:, :] = total
    w_out[...] = total


def sum_of_four(parts):
    return (f32(parts[0]) + f32(parts[2])) + (f32(parts[1]) + f32(parts[3]))


def assemble_kernel(me_ref, own_ref, other_ref, out_ref):
    parts = out_ref.shape[1] // TILE
    rows = own_ref.shape[0] // X // parts
    for s in range(X):
        first = (me_ref[0] + s & 3) * C * rows
        for ref, core in ((own_ref, me_ref[1]), (other_ref, 1 - me_ref[1])):
            place = pl.ds(pl.multiple_of(first + core * rows, rows), rows)
            for i in range(parts):
                start = (s * parts + i) * rows
                out_ref[place, i * TILE : (i + 1) * TILE] = ref[start : start + rows, :]


def body(node_features, tile_coords, tile_count, tile_values, weight, cotangent):
    features = node_features[0]
    me_row = lax.axis_index("row")
    me_col = lax.axis_index("col")
    my, mz = me_row >> 2, me_row & 3
    mx, mh, mk = me_col >> 2, me_col >> 1 & 1, me_col & 1
    nodes_all = TILE * Y * Z * X * H * C
    full = features.shape[1]

    tr, tc = tile_coords[0, 0, 0], tile_coords[0, 0, 1]
    place_r = ((tr >> 1) + mh & 1) * 8 + (tr + mk & 1) * 4 + ((tr >> 2) - mx & 3)
    far_y, far_z = (tc >> 2) - my & 3, tc - mz & 3
    place_c = jnp.where(
        far_y == 0, far_z, jnp.where(far_z == 0, 3 + far_y, 3 + far_y * 3 + far_z)
    )
    place = jnp.stack([place_r, place_c])
    values, count = tile_values[0, 0], tile_count[0]

    along_y = from_y(features)
    along_z, along_y[1], forward = join(
        from_z(features), along_y[1], densify(values, place, count, (0, 7), (7, 16))
    )
    rest = jnp.concatenate(along_z)
    near = jnp.concatenate([features, rest] + along_y)
    far = [row_shift(rest, "y", 1), row_shift(rest, "y", 3)]
    far += [row_shift(along_y[1], "z", 1), row_shift(along_y[1], "z", 3)]
    far += [row_shift(along_z[1], "y", 2)]
    far, near = join(far, products(forward[0], near, None, TILE, [(0, 16, F32)])[0])
    far = jnp.concatenate([far[0], far[2], far[4], far[3], far[1]])

    (away,) = products(forward[1], far, near, 512, [(12, 16, BF16)])
    away, far = join(away, far)
    arrived = col_shift(away, "k", 1)
    (rest,) = products(forward[1], far, near, 512, [(0, 12, F32)])
    home, away, own = rows_of(rest, 8, 12), bf16(rows_of(rest, 4, 8)), rows_of(rest, 0, 4)
    home, arrived, away, own = join(home, arrived, away, own)
    lead = [bf16(rows_of(home, s, s + 1) + f32(rows_of(arrived, s, s + 1))) for s in range(X)]
    lead_parts = [col_shift(lead[s], "x", X - s) for s in (1, 2, 3)]
    lead, arrived = lead[0], col_shift(away, "k", 1)
    lead = bf16(total_of(lead, lead_parts))
    own = [rows_of(own, s, s + 1) + f32(rows_of(arrived, s, s + 1)) for s in range(X)]
    lead = col_shift(lead, "h", 1)
    own_parts = [col_shift(bf16(own[s]), "x", X - s) for s in (1, 2, 3)]
    me = jnp.stack([mx, mk])
    wider = full + TILE
    hidden, both, *own_sent = call(
        middle_kernel,
        [((TILE, full), BF16), ((2 * full, TILE), BF16)] + [((wider, TILE), BF16)] * X,
        me,
        own[0],
        lead,
        *own_parts,
        weight,
        cotangent[0],
        scalars=1,
        flops=2 * TILE * full * full,
    )

    other = col_shift(both, "h", 1)
    own_parts = [col_shift(own_sent[s], "x", s) for s in (1, 2, 3)]
    other, own_parts = join(other, own_parts)
    own = jnp.concatenate([own_sent[0]] + own_parts, axis=1)
    other_sent = call(split_kernel, [((wider, TILE), BF16)] * X, me, other, scalars=1)
    own_core = col_shift(own, "k", 1)
    other_parts = [col_shift(other_sent[s], "x", s) for s in (1, 2, 3)]
    first = jnp.concatenate([own, own_core], axis=1)
    near, far, w_first = call(
        first_kernel,
        [((full, 7 * TILE), F32), ((full, 9 * TILE), F32), ((TILE, full), F32)],
        *forward,
        first,
        flops=2 * 16 * TILE * full * 8 * TILE,
    )
    other_parts, near, far, w_first = join(other_parts, near, far, w_first)
    other = jnp.concatenate([other_sent[0]] + other_parts, axis=1)
    source = jnp.concatenate([other, col_shift(other, "k", 1)], axis=1)

    rows = full * full // (X * C) // TILE
    lead1, over1, lead2, over3, lead3, w = call(
        lead_kernel,
        [((full, 3 * TILE), BF16), ((full + rows, TILE), BF16), ((full, TILE), BF16)]
        + [((full + rows, TILE), BF16), ((full, 3 * TILE), BF16), ((rows, TILE), BF16)],
        me,
        forward[1],
        source,
        w_first,
        far,
        scratch=[pltpu.VMEM((TILE, full), F32)],
        scalars=1,
        flops=2 * 9 * TILE * full * 8 * TILE,
    )
    near1, near2, near3, run, own, pair = call(
        rest_kernel,
        [((full, TILE), BF16), ((full, TILE), F32), ((full, TILE), BF16)]
        + [((full, 3 * TILE), F32), ((full, TILE), F32), ((rows, TILE), F32)],
        forward[0],
        source,
        near,
        row_shift(lead2, "y", 2),
        w,
        row_shift(w, "z", 2),
        flops=2 * 7 * TILE * full * 8 * TILE,
    )
    parts = join(
        row_shift(lead1, "y", 3),
        row_shift(lead3, "y", 1),
        row_shift(over1, "z", 3),
        row_shift(over3, "z", 1),
    )
    *run, near1, near2, near3, w = call(
        combine_kernel,
        [((full, TILE), BF16)] * 3 + [((full + rows, TILE), BF16)] * 3 + [((rows, TILE), BF16)],
        run,
        near1,
        near2,
        near3,
        pair,
        *parts,
    )
    z_parts = [row_shift(run[s - 1], "z", Z - s) for s in (1, 2, 3)]
    near_parts = [
        row_shift(near, "y", Y - s) for s, near in ((1, near1), (2, near2), (3, near3))
    ]
    z_parts, near_parts = join(z_parts, near_parts)
    w = bf16(sum_of_four([w] + [part[full:] for part in near_parts]))
    (w,) = join(w)
    w_parts = from_x(w)
    back = bf16(total_of(own, [part[:full] for part in near_parts] + z_parts))
    feature_grad = bf16(
        lax.dot_general(
            back, weight, (((0,), (1,)), ((), ())), preferred_element_type=jnp.float32
        )
    )

    parts = jnp.concatenate([w] + w_parts)
    (w,) = call(
        assemble_kernel, [((full, full), BF16)], me, parts, col_shift(parts, "k", 1), scalars=1
    )
    weight_grad = f32(w) / math.sqrt(nodes_all)
    return (hidden[None], weight_grad, feature_grad[None])


def solution(mesh):
    in_specs = (
        P("col", "row", None),
        P("row", "col", None, None),
        P("row", "col"),
        P("row", "col", None, None, None),
        P(),
        P("row", "col", None),
    )
    out_specs = (P("row", "col", None), P(), P("col", "row", None))
    return jax.shard_map(body, mesh=mesh, in_specs=in_specs, out_specs=out_specs, check_vma=False)
```
